512 devices in a mesh: gx: 32 (over x, y, core), gy: 4 (over z_hi), gz: 4 (over z_lo).
Axes of the slice: x: 4, y: 4, z: 16 (z_hi: 4, z_lo: 4; z = z_hi * 4 + z_lo), core: 2. Of those that a mesh axis runs over, the one named last changes fastest.
Arguments:
- feats: bfloat16 [65536, 128], P(('gx', 'gy', 'gz')), may hold values from -6 to 6
- coords: float32 [3, 65536], P(None, ('gx', 'gy', 'gz')), may hold values from 0 to 1, as said below
- pair_dist: float32 [65536, 64], P(('gx', 'gy', 'gz')), may hold values from 0.9 to 5
- nbr_index: int32 [65536, 64], P(('gx', 'gy', 'gz')), may hold values from 0 to 703, as said below
- nbr_count: int32 [65536], P(('gx', 'gy', 'gz')), may hold values from 8 to 64
- send_x: int32 [2, 32768], P(None, ('gx', 'gy', 'gz')), may hold values from 0 to 127, as said below
- send_y: int32 [2, 49152], P(None, ('gx', 'gy', 'gz')), may hold values from 0 to 255, as said below
- send_z: int32 [2, 65536], P(None, ('gx', 'gy', 'gz')), may hold values from 0 to 447, as said below
- w_one: bfloat16 [128, 128], replicated, may hold values from -0.5 to 0.5
- w_two: bfloat16 [128, 128], replicated, may hold values from -0.5 to 0.5
- w_radial: bfloat16 [20, 128], replicated, may hold values from -1.25 to 1.25
- w_charge: bfloat16 [128, 32], replicated, may hold values from -0.5 to 0.5
- k_kernel: float32 [1024, 32], replicated, may hold values from 0.2 to 2
- w_ewald: bfloat16 [32, 128], replicated, may hold values from -1 to 1
Outputs:
- update: bfloat16 [65536, 128], P(('gx', 'gy', 'gz'))
The draws below stay inside these ranges and needn't reach their ends.
Inputs may be any that keep to these rules, and one draw needn't show every extreme that they name: Each subdomain's atoms lie in its box: coords[0] of subdomain (a, b, c) is within a / 32 and (a + 1) / 32, likewise for the other two. `nbr_index`: entries are rows of the atom's subdomain table; entries at slots nbr_count[i] and beyond are padding. `send_x`: within one row of a subdomain's columns no entry repeats. `send_y`: within one row of a subdomain's columns no entry repeats. `send_z`: within one row of a subdomain's columns no entry repeats.
All inputs are finite; a program needn't handle non-finite values.
Results may differ from the reference program's by a relative error of at most 0.009.
Values may be sent and summed in bfloat16 or wider, within the bound.
No kernel may reach another device: no remote copies, remote signals or barrier semaphores. Data moves between devices by JAX's collectives and lax.ppermute only.
A program may use at most 64 MiB of HBM per device.

```python
import math
import jax
import jax.numpy as jnp
from jax import lax

FEAT = 128
CHARGES = 32
KVECS = 1024
RADIAL = 20
SLOTS = 64
ATOM_DEV = 128
SPLIT_X = 32
SPLIT_Y = 4
SPLIT_Z = 4
SUBDOMAINS = 512
ATOMS = 65536
GHOST_X = 64
GHOST_Y = 96
GHOST_Z = 128
EXTENDED = 704
N_GX = 32
N_GY = 4
N_GZ = 4


def choose_rows(key, side_count, source_size, amount):
    subkeys = jax.random.split(key, side_count * SUBDOMAINS)
    chosen = jax.vmap(lambda subkey: jax.random.permutation(subkey, source_size)[:amount])(subkeys)
    return chosen.reshape(side_count, SUBDOMAINS * amount).astype(jnp.int32)


def draw_coords(key, part):
    key = jax.random.fold_in(key, 5)
    owner = jnp.arange(ATOMS, dtype=jnp.int32) // ATOM_DEV
    grid_first = owner // (SPLIT_Y * SPLIT_Z)
    grid_second = owner // SPLIT_Z % SPLIT_Y
    grid_third = owner % SPLIT_Z
    offsets = jax.random.uniform(key, (3, ATOMS), jnp.float32)
    corner = jnp.stack([grid_first, grid_second, grid_third]).astype(jnp.float32)
    splits = jnp.array([SPLIT_X, SPLIT_Y, SPLIT_Z], jnp.float32)[:, None]
    return (corner + offsets) / splits


def draw_nbr_index(key, part):
    key = jax.random.fold_in(key, 11)
    key_own, key_ghost, key_pick = jax.random.split(key, 3)
    shape_all = (ATOMS, SLOTS)
    owned = jax.random.randint(key_own, shape_all, 0, ATOM_DEV)
    ghostly = jax.random.randint(key_ghost, shape_all, ATOM_DEV, EXTENDED)
    chooser = jax.random.randint(key_pick, shape_all, 0, 10)
    return jnp.where(chooser < 7, owned, ghostly).astype(jnp.int32)


def draw_send_x(key, part):
    key = jax.random.fold_in(key, 21)
    return choose_rows(key, 2, ATOM_DEV, GHOST_X)


def draw_send_y(key, part):
    key = jax.random.fold_in(key, 22)
    return choose_rows(key, 2, ATOM_DEV + 2 * GHOST_X, GHOST_Y)


def draw_send_z(key, part):
    key = jax.random.fold_in(key, 23)
    return choose_rows(key, 2, ATOM_DEV + 2 * GHOST_X + 2 * GHOST_Y, GHOST_Z)


def place_ends(values, rng, least, largest):
    longest = values.shape.index(max(values.shape))
    spots = []
    for shift in (0, 1):
        where = [jax.random.randint(jax.random.fold_in(rng, axis), (), 0, length) for axis, length in enumerate(values.shape)]
        where[longest] = (where[longest] + shift) % values.shape[longest]
        spots.append(tuple(where))
    return values.at[spots[0]].set(least).at[spots[1]].set(largest)


def shard_levels(stream_key, shape, cuts, least, top_value):
    level, own = 1.0, jax.random.fold_in(stream_key, 6)
    for dim, blocks in cuts:
        heights = jnp.exp(jax.random.uniform(jax.random.fold_in(own, dim), (blocks,), jnp.float32, least / len(cuts), top_value / len(cuts)))
        level = level * jnp.repeat(heights, shape[dim] // blocks).reshape([-1 if axis == dim else 1 for axis in range(len(shape))])
    return level


def gaussian(stream_key, dims, scale, limit, cuts=(), held_as=jnp.bfloat16):
    gain = shard_levels(stream_key, dims, cuts, -0.22, 0.18) if cuts else 1.0
    drawn = jax.random.normal(stream_key, dims, jnp.float32) * scale * gain
    return jnp.minimum(jnp.maximum(drawn, -limit), limit).astype(held_as)


def setup_inputs(seed: int = 0) -> dict:
    key_of = jax.random.split(jax.random.key(seed), 15)
    return {
        "feats": gaussian(key_of[0], (ATOMS, FEAT), 1.0, 6.0, ((0, 512),)),
        "coords": draw_coords(jax.random.fold_in(key_of[14], 71), 0),
        "pair_dist": jnp.clip(0.9 + 4.1 * jax.random.uniform(key_of[2], (ATOMS, SLOTS), jnp.float32) ** shard_levels(key_of[2], (ATOMS, SLOTS), ((0, 512),), -0.2, 0.2), 0.9, 5.0),
        "nbr_index": draw_nbr_index(jax.random.fold_in(key_of[14], 71), 0),
        "nbr_count": place_ends(jax.random.randint(key_of[4], (ATOMS,), SLOTS // 8, SLOTS + 1), jax.random.fold_in(key_of[4], 1), SLOTS // 8, SLOTS).astype(jnp.int32),
        "send_x": draw_send_x(jax.random.fold_in(key_of[14], 71), 0),
        "send_y": draw_send_y(jax.random.fold_in(key_of[14], 71), 0),
        "send_z": draw_send_z(jax.random.fold_in(key_of[14], 71), 0),
        "w_one": gaussian(key_of[8], (FEAT, FEAT), FEAT ** -0.5, 0.5),
        "w_two": gaussian(key_of[9], (FEAT, FEAT), FEAT ** -0.5, 0.5),
        "w_radial": gaussian(key_of[10], (RADIAL, FEAT), RADIAL ** -0.5, 1.25),
        "w_charge": gaussian(key_of[11], (FEAT, CHARGES), FEAT ** -0.5, 0.5),
        "k_kernel": jnp.clip(jnp.exp(jax.random.uniform(key_of[12], (KVECS, CHARGES), jnp.float32, math.log(0.2), math.log(2.0))), 0.2, 2.0),
        "w_ewald": gaussian(key_of[13], (CHARGES, FEAT), CHARGES ** -0.5, 1.0),
    }


cutoff = 5.0
pair_scale = 0.25

def wave_numbers(total):
    k_index = jnp.arange(total, dtype=jnp.int32)
    along_third = (k_index % 8 + 1).astype(jnp.float32)
    along_second = (k_index // 8 % 8 - 4).astype(jnp.float32)
    along_first = (k_index // 64 - total // 64 // 2).astype(jnp.float32)
    return (along_first, along_second, along_third)

def trig_tables(coords, total):
    along_first, along_second, along_third = wave_numbers(total)
    phase = along_first[:, None] * coords[0][None, :] + along_second[:, None] * coords[1][None, :] + along_third[:, None] * coords[2][None, :]
    angle = 2.0 * math.pi * phase
    return (jnp.cos(angle).astype(jnp.bfloat16), jnp.sin(angle).astype(jnp.bfloat16))

def pair_filter(distance, w_radial):
    orders = jnp.arange(1, w_radial.shape[0] + 1, dtype=jnp.int32).astype(jnp.float32)
    radial_basis = (jnp.sin(orders[:, None] * (math.pi / cutoff) * distance[None, :]) / distance[None, :]).astype(jnp.bfloat16)
    radial = lax.dot_general(radial_basis, w_radial, (((0,), (0,)), ((), ())), preferred_element_type=jnp.float32)
    envelope = 0.5 * (jnp.cos(math.pi / cutoff * distance) + 1.0)
    return (radial * envelope[:, None]).astype(jnp.bfloat16)

def message_base(feats, w_one, w_two):
    hidden = jax.nn.silu(jnp.dot(feats, w_one, preferred_element_type=jnp.float32)).astype(jnp.bfloat16)
    return jnp.dot(hidden, w_two, preferred_element_type=jnp.float32).astype(jnp.bfloat16)

def charges_of(feats, w_charge):
    return lax.dot_general(w_charge, feats, (((0,), (1,)), ((), ())), preferred_element_type=jnp.float32).astype(jnp.bfloat16)

def structure_terms(cos_table, sin_table, charge_t):
    real_part = lax.dot_general(cos_table, charge_t, (((1,), (1,)), ((), ())), preferred_element_type=jnp.float32)
    imag_part = lax.dot_general(sin_table, charge_t, (((1,), (1,)), ((), ())), preferred_element_type=jnp.float32)
    return jnp.concatenate([real_part, imag_part], axis=1)

def potential(factors, cos_table, sin_table, total):
    channels = factors.shape[1] // 2
    real_part = lax.dot_general(factors[:, :channels], cos_table, (((0,), (0,)), ((), ())), preferred_element_type=jnp.float32)
    imag_part = lax.dot_general(factors[:, channels:], sin_table, (((0,), (0,)), ((), ())), preferred_element_type=jnp.float32)
    return ((real_part + imag_part) * (1.0 / math.sqrt(total))).astype(jnp.bfloat16)

def take_rows(tables, indices):
    return jax.vmap(lambda one_table, one_index: one_table[one_index])(tables, indices)

def add_rows(tables, indices, values):
    return jax.vmap(lambda one_table, one_index, one_value: one_table.at[one_index].add(one_value))(tables, indices, values)

def neighbour_rims(packet, grid_shape, axis_number):
    rim_rows = packet.shape[1] // 2
    subdomain_count = packet.shape[0]
    shaped = packet.reshape(grid_shape + packet.shape[1:])
    from_below = jnp.roll(shaped, 1, axis=axis_number)[:, :, :, rim_rows:]
    from_above = jnp.roll(shaped, -1, axis=axis_number)[:, :, :, :rim_rows]
    tail_shape = (subdomain_count, rim_rows) + packet.shape[2:]
    return (from_below.reshape(tail_shape), from_above.reshape(tail_shape))

def pair_terms(ext_table, distance, partner, listed, w_radial):
    atom_count, slot_count = distance.shape
    feature_count = ext_table.shape[1]
    radial_terms = pair_filter(distance.reshape(-1), w_radial).astype(jnp.float32)
    filled = (jnp.arange(slot_count, dtype=jnp.int32)[None, :] < listed[:, None]).reshape(-1)
    flat_partner = partner.reshape(-1)
    partner_rows = ext_table[flat_partner].astype(jnp.float32)
    inward = jnp.where(filled[:, None], partner_rows * radial_terms, 0.0)
    gathered = lax.optimization_barrier(jnp.sum(inward.reshape(atom_count, slot_count, feature_count), axis=1))
    own_rows = ext_table[:atom_count].astype(jnp.float32)
    outward = (radial_terms.reshape(atom_count, slot_count, feature_count) * own_rows[:, None, :]).reshape(-1, feature_count)
    outward = jnp.where(filled[:, None], outward, 0.0)
    spread = jnp.zeros(ext_table.shape, jnp.float32).at[flat_partner].add(outward)
    return (gathered, spread)

def reference(feats, coords, pair_dist, nbr_index, nbr_count, send_x, send_y, send_z, w_one, w_two, w_radial, w_charge, k_kernel, w_ewald):
    grid_shape = (N_GX, N_GY, N_GZ)
    subdomain_count = N_GX * N_GY * N_GZ
    feature_count = feats.shape[1]
    base = message_base(feats, w_one, w_two).reshape(subdomain_count, ATOM_DEV, feature_count)
    send_lists = [send_rows.reshape(2, subdomain_count, -1) for send_rows in (send_x, send_y, send_z)]
    ext_table = base
    for axis_number in range(3):
        send_rows = send_lists[axis_number]
        packet = jnp.concatenate([take_rows(ext_table, send_rows[0]), take_rows(ext_table, send_rows[1])], axis=1)
        from_below, from_above = neighbour_rims(packet, grid_shape, axis_number)
        ext_table = jnp.concatenate([ext_table, from_below, from_above], axis=1)
    packed_inputs = (ext_table, pair_dist.reshape(subdomain_count, ATOM_DEV, -1), nbr_index.reshape(subdomain_count, ATOM_DEV, -1), nbr_count.reshape(subdomain_count, ATOM_DEV))
    gathered, spread = lax.map(lambda packed: pair_terms(packed[0], packed[1], packed[2], packed[3], w_radial), packed_inputs)
    offsets = [ATOM_DEV, ATOM_DEV + 2 * GHOST_X, ATOM_DEV + 2 * GHOST_X + 2 * GHOST_Y]
    for axis_number in (2, 1, 0):
        send_rows = send_lists[axis_number]
        offset = offsets[axis_number]
        rim_rows = send_rows.shape[2]
        packet = spread[:, offset:offset + 2 * rim_rows].astype(jnp.bfloat16)
        from_below, from_above = neighbour_rims(packet, grid_shape, axis_number)
        spread = spread[:, :offset]
        spread = add_rows(spread, send_rows[1], from_below.astype(jnp.float32))
        spread = add_rows(spread, send_rows[0], from_above.astype(jnp.float32))
    pair_update = ((gathered + spread) * pair_scale).reshape(ATOMS, feature_count)
    coords_split = coords.reshape(3, subdomain_count, ATOM_DEV).transpose(1, 0, 2)
    feats_split = feats.reshape(subdomain_count, ATOM_DEV, feature_count)

    def partial_structure(packed):
        cos_table, sin_table = trig_tables(packed[0], KVECS)
        return structure_terms(cos_table, sin_table, charges_of(packed[1], w_charge))
    structure = lax.optimization_barrier(jnp.sum(lax.map(partial_structure, (coords_split, feats_split)), axis=0))
    doubled = jnp.concatenate([k_kernel, k_kernel], axis=1)
    factors = (structure * doubled * (1.0 / math.sqrt(ATOMS))).astype(jnp.bfloat16)

    def project(sub_coords):
        cos_table, sin_table = trig_tables(sub_coords, KVECS)
        field = potential(factors, cos_table, sin_table, KVECS)
        return lax.dot_general(field, w_ewald, (((0,), (0,)), ((), ())), preferred_element_type=jnp.float32)
    ewald_update = lax.map(project, coords_split).reshape(ATOMS, feature_count)
    return (pair_update + ewald_update).astype(jnp.bfloat16)
```

```python
import math

import jax
import jax.numpy as jnp
from jax import lax
from jax.experimental import pallas as pl
from jax.experimental.pallas import tpu as pltpu
from jax.sharding import PartitionSpec as P

cutoff = 5.0
pair_scale = 0.25
basis_rows = 32
slot_group = 4
gather_group = 8
mebi = 1024 * 1024


def kernel_call(body, outs, operands, flops, limit, scratch=(), scalars=0):
    specs = [pl.BlockSpec(memory_space=pltpu.SMEM)] * scalars
    specs += [pl.BlockSpec(memory_space=pltpu.VMEM)] * (len(operands) - scalars)
    moved = sum(math.prod(v.shape) * v.dtype.itemsize for v in (*operands, *outs))
    return pl.pallas_call(
        body,
        out_shape=tuple(outs),
        in_specs=specs,
        out_specs=(pl.BlockSpec(memory_space=pltpu.VMEM),) * len(outs),
        scratch_shapes=list(scratch),
        compiler_params=pltpu.CompilerParams(vmem_limit_bytes=limit * mebi),
        cost_estimate=pl.CostEstimate(flops=flops, bytes_accessed=moved, transcendentals=0),
    )(*operands)


def like(shape, dtype):
    return jax.ShapeDtypeStruct(shape, dtype)


def dot32(left, right):
    return jnp.dot(left, right, preferred_element_type=jnp.float32)


def picked(send, side, table):
    columns = jnp.concatenate([send] * 4, axis=0).T[:, side : side + 1]
    lanes = lax.broadcasted_iota(jnp.int32, (send.shape[1], table.shape[0]), 1)
    return dot32((columns == lanes).astype(jnp.bfloat16), table).astype(jnp.bfloat16)


def placed(send, below, above, rows):
    iota = lax.broadcasted_iota(jnp.int32, (rows, send.shape[1]), 0)
    low = dot32((iota == send[1:2]).astype(jnp.bfloat16), below)
    return low + dot32((iota == send[0:1]).astype(jnp.bfloat16), above)


def base_body(feats_ref, one_ref, two_ref, send_ref, base_ref, low_ref, high_ref):
    raw = dot32(feats_ref[...], one_ref[...])
    hidden = (raw / (1.0 + jnp.exp(-raw))).astype(jnp.bfloat16)
    base = dot32(hidden, two_ref[...]).astype(jnp.bfloat16)
    base_ref[...] = base
    low_ref[...] = picked(send_ref[...], 0, base)
    high_ref[...] = picked(send_ref[...], 1, base)


def extend_body(*refs):
    *parts, send_ref, low_ref, high_ref = refs
    table = jnp.concatenate([part[...] for part in parts], axis=0)
    low_ref[...] = picked(send_ref[...], 0, table)
    high_ref[...] = picked(send_ref[...], 1, table)


def fold_body(spread_ref, below_ref, above_ref, send_ref, core_ref, low_ref, high_ref):
    rows = spread_ref.shape[0]
    keep = core_ref.shape[0]
    half = low_ref.shape[0]
    total = spread_ref[...] + placed(send_ref[...], below_ref[...], above_ref[...], rows)
    core_ref[...] = total[:keep]
    low_ref[...] = total[keep : keep + half].astype(jnp.bfloat16)
    high_ref[...] = total[keep + half :].astype(jnp.bfloat16)


def unit_waves(coord, first, count):
    orders = (lax.broadcasted_iota(jnp.int32, (count, coord.shape[1]), 0) + first).astype(jnp.float32)
    turns = orders * coord
    angle = (2.0 * math.pi) * (turns - jnp.round(turns))
    return jnp.cos(angle), jnp.sin(angle)


def outer_waves(left, right):
    left_cos, left_sin = (v[:, None, :] for v in left)
    right_cos, right_sin = (v[None, :, :] for v in right)
    shape = (left_cos.shape[0] * right_cos.shape[1], left_cos.shape[2])
    cos_part = (left_cos * right_cos - left_sin * right_sin).reshape(shape)
    return cos_part, (left_sin * right_cos + left_cos * right_sin).reshape(shape)


def wave_body(coords_ref, feats_ref, charge_ref, blocks_ref, cos_ref, sin_ref):
    total, atoms = cos_ref.shape
    firsts = total // 64
    coords = coords_ref[...]
    along_first = unit_waves(coords[0:1], -(firsts // 2), firsts)
    along_second = unit_waves(coords[1:2], -4, 8)
    along_third = unit_waves(coords[2:3], 1, 8)
    cos_part, sin_part = outer_waves(outer_waves(along_first, along_second), along_third)
    cos_table = cos_part.astype(jnp.bfloat16)
    sin_table = sin_part.astype(jnp.bfloat16)
    cos_ref[...] = cos_table
    sin_ref[...] = sin_table
    charge_t = dot32(feats_ref[...], charge_ref[...]).T.astype(jnp.bfloat16)
    over_atoms = (((1,), (1,)), ((), ()))
    real = lax.dot_general(charge_t, cos_table, over_atoms, preferred_element_type=jnp.float32)
    imag = lax.dot_general(charge_t, sin_table, over_atoms, preferred_element_type=jnp.float32)
    blocks, height, width = blocks_ref.shape
    both = jnp.concatenate([real, imag], axis=0).astype(blocks_ref.dtype)
    across = total // width
    for block in range(blocks):
        down, along = block // across * height, block % across * width
        blocks_ref[block] = both[down : down + height, along : along + width]


def merge_body(parts_ref, copies_ref):
    total = jnp.sum(parts_ref[...].astype(jnp.float32), axis=0)
    copies_ref[...] = jnp.broadcast_to(total.astype(copies_ref.dtype)[None], copies_ref.shape)


def factor_body(where_ref, parts_ref, kernel_ref, copies_ref, norm_factor):
    blocks, height, width = copies_ref.shape
    across = kernel_ref.shape[0] // width
    down, along = where_ref[0] // across, where_ref[0] % across
    start = pl.multiple_of(along * width, width)
    weights = kernel_ref[pl.ds(start, width), :].T
    weights = jnp.where(down % 2 == 0, weights[:height], weights[height:])
    total = jnp.sum(parts_ref[...].astype(jnp.float32), axis=0)
    factors = (total * weights * norm_factor).astype(copies_ref.dtype)
    copies_ref[...] = jnp.broadcast_to(factors[None], copies_ref.shape)


def spread_body(
    dist_ref, nbr_ref, count_ref, base_ref, wide_ref,
    core_ref, low_ref, high_ref, radial_ref, basis_ref, partner_ref, total_ref,
):
    atoms, slots = dist_ref.shape
    feat = base_ref.shape[1]
    core, half = core_ref.shape[0], low_ref.shape[0]
    distance = dist_ref[...].T
    partner_ref[...] = nbr_ref[...].T
    angle = (math.pi / cutoff) * distance
    turn = jnp.cos(angle)
    listed = lax.broadcasted_iota(jnp.int32, (slots, atoms), 0) < count_ref[...]
    fade = jnp.where(listed, 0.5 * (turn + 1.0), 0.0) / distance
    turn = turn + turn
    basis_ref[...] = jnp.zeros_like(basis_ref)
    before, now = jnp.zeros_like(angle), jnp.sin(angle)
    for order in range(20):
        term = now * fade
        for row in range(0, slots, 8):
            place = pl.ds(row * basis_rows + order, 8, stride=basis_rows)
            basis_ref[place, :] = term[row : row + 8]
        before, now = now, turn * now - before
    total_ref[...] = jnp.zeros_like(total_ref)
    base = base_ref[...]
    iota = lax.broadcasted_iota(jnp.int32, (total_ref.shape[0], atoms), 0)
    group_rows = slot_group * basis_rows

    def step(index, carry):
        start = pl.multiple_of(index * group_rows, group_rows)
        block = basis_ref[pl.ds(start, group_rows), :].T.astype(jnp.bfloat16)
        wide = dot32(block, wide_ref[...]).astype(jnp.bfloat16)
        pickers, outward = [], []
        for offset in range(slot_group):
            slot = index * slot_group + offset
            radial = wide[:, offset * feat : (offset + 1) * feat]
            radial_ref[slot] = radial
            outward.append(radial * base)
            pickers.append((iota == partner_ref[pl.ds(slot, 1), :]).astype(jnp.bfloat16))
        picker = jnp.concatenate(pickers, axis=1)
        total_ref[...] += dot32(picker, jnp.concatenate(outward, axis=0))
        return carry

    lax.fori_loop(0, slots // slot_group, step, 0)
    core_ref[...] = total_ref[:core]
    low_ref[...] = total_ref[core : core + half].astype(jnp.bfloat16)
    high_ref[...] = total_ref[core + half :].astype(jnp.bfloat16)


def gather_body(nbr_ref, radial_ref, *refs):
    *parts, gathered_ref = refs
    atoms, slots = nbr_ref.shape
    table = jnp.concatenate([part[...] for part in parts], axis=0)
    lanes = lax.broadcasted_iota(jnp.int32, (atoms, table.shape[0]), 1)
    spare = jnp.zeros((atoms, 128 - slots), jnp.int32)

    def step(index, state):
        partner, total = state
        for offset in range(gather_group):
            picker = (partner[:, offset : offset + 1] == lanes).astype(jnp.bfloat16)
            rows = dot32(picker, table)
            radial = radial_ref[index * gather_group + offset].astype(jnp.float32)
            total = total + rows * radial
        return pltpu.roll(partner, 128 - gather_group, 1), total

    start = (jnp.concatenate([nbr_ref[...], spare], axis=1), jnp.zeros(gathered_ref.shape, jnp.float32))
    gathered_ref[...] = lax.fori_loop(0, slots // gather_group, step, start)[1]


def update_body(
    spread_ref, below_ref, above_ref, send_ref, gathered_ref, factor_ref, cos_ref, sin_ref, ewald_ref, out_ref
):
    atoms = spread_ref.shape[0]
    returned = spread_ref[...] + placed(send_ref[...], below_ref[...], above_ref[...], atoms)
    pair_update = (gathered_ref[...] + returned) * pair_scale
    total = cos_ref.shape[0]
    blocks, height, width = factor_ref.shape
    across = total // width
    lines = []
    for down in range(blocks // across):
        lines.append(jnp.concatenate([factor_ref[down * across + i] for i in range(across)], axis=1))
    real = dot32(jnp.concatenate(lines[: len(lines) // 2], axis=0), cos_ref[...])
    imag = dot32(jnp.concatenate(lines[len(lines) // 2 :], axis=0), sin_ref[...])
    field = ((real + imag) * (1.0 / math.sqrt(total))).T.astype(jnp.bfloat16)
    out_ref[...] = (pair_update + dot32(field, ewald_ref[...])).astype(out_ref.dtype)


def swap(low, high, axis):
    count = lax.axis_size(axis)
    forward = [(i, (i + 1) % count) for i in range(count)]
    backward = [(target, source) for source, target in forward]
    return lax.ppermute(high, axis, forward), lax.ppermute(low, axis, backward)


def on_device(
    feats,
    coords,
    pair_dist,
    nbr_index,
    nbr_count,
    send_x,
    send_y,
    send_z,
    w_one,
    w_two,
    w_radial,
    w_charge,
    k_kernel,
    w_ewald,
):
    atoms, feat = feats.shape
    slots = pair_dist.shape[1]
    charges = w_charge.shape[1]
    total = k_kernel.shape[0]
    rim_x, rim_y, rim_z = send_x.shape[1], send_y.shape[1], send_z.shape[1]
    with_x = atoms + 2 * rim_x
    with_y = with_x + 2 * rim_y
    with_z = with_y + 2 * rim_z
    half, full = jnp.bfloat16, jnp.float32
    count_x = lax.axis_size("gx")
    count_yz = lax.axis_size("gy") * lax.axis_size("gz")
    across = total // 128
    height = 2 * charges * across // count_x

    base, low, high = kernel_call(
        base_body,
        (like((atoms, feat), half), like((rim_x, feat), half), like((rim_x, feat), half)),
        (feats, w_one, w_two, send_x), 10**7, 8,
    )
    below_x, above_x = swap(low, high, "gx")
    blocks, cos_table, sin_table = kernel_call(
        wave_body,
        (like((count_x, height, 128), half), like((total, atoms), half), like((total, atoms), half)),
        (coords, feats, w_charge), 10**8, 16,
    )
    parts = lax.all_to_all(blocks, "gx", split_axis=0, concat_axis=0)

    padded = jnp.pad(w_radial, ((0, basis_rows - w_radial.shape[0]), (0, 0)))
    wide = jnp.kron(jnp.eye(slot_group, dtype=half), padded)
    core, low, high, radial = kernel_call(
        spread_body,
        (
            like((with_y, feat), full), like((rim_z, feat), half), like((rim_z, feat), half),
            like((slots, atoms, feat), half),
        ),
        (pair_dist, nbr_index, nbr_count[None, :], base, wide), 3 * 10**9, 24,
        (
            pltpu.VMEM((slots * basis_rows, atoms), full), pltpu.VMEM((slots, atoms), jnp.int32),
            pltpu.VMEM((with_z, feat), full),
        ),
    )
    below, above = swap(low, high, "gz")

    low, high = kernel_call(
        extend_body, (like((rim_y, feat), half),) * 2, (base, below_x, above_x, send_y), 10**7, 8
    )
    below_y, above_y = swap(low, high, "gy")
    (copies,) = kernel_call(
        merge_body, (like((count_yz, height, 128), half),), (parts,), 10**6, 8
    )
    parts = lax.all_to_all(copies, ("gy", "gz"), split_axis=0, concat_axis=0)

    core, low, high = kernel_call(
        fold_body,
        (like((with_x, feat), full), like((rim_y, feat), half), like((rim_y, feat), half)),
        (core, below, above, send_z), 10**7, 8,
    )
    below, above = swap(low, high, "gy")
    low, high = kernel_call(
        extend_body, (like((rim_z, feat), half),) * 2, (base, below_x, above_x, below_y, above_y, send_z), 10**7, 8
    )
    below_z, above_z = swap(low, high, "gz")

    norm_factor = 1.0 / math.sqrt(atoms * count_x * count_yz)
    where = lax.axis_index("gx").astype(jnp.int32)[None]
    (copies,) = kernel_call(
        lambda *refs: factor_body(*refs, norm_factor),
        (like((count_x, height, 128), half),), (where, parts, k_kernel), 10**6, 8, scalars=1,
    )
    factors = lax.all_to_all(copies, "gx", split_axis=0, concat_axis=0)

    core, low, high = kernel_call(
        fold_body,
        (like((atoms, feat), full), like((rim_x, feat), half), like((rim_x, feat), half)),
        (core, below, above, send_y), 10**7, 8,
    )
    below, above = swap(low, high, "gx")
    (gathered,) = kernel_call(
        gather_body, (like((atoms, feat), full),),
        (nbr_index, radial, base, below_x, above_x, below_y, above_y, below_z, above_z), 15 * 10**8, 24,
    )
    (update,) = kernel_call(
        update_body, (like((atoms, feat), half),),
        (core, below, above, send_x, gathered, factors, cos_table, sin_table, w_ewald), 10**8, 16,
    )
    return update


def solution(mesh):
    in_specs = (
        P(("gx", "gy", "gz"), None),
        P(None, ("gx", "gy", "gz")),
        P(("gx", "gy", "gz"), None),
        P(("gx", "gy", "gz"), None),
        P(("gx", "gy", "gz")),
        P(None, ("gx", "gy", "gz")),
        P(None, ("gx", "gy", "gz")),
        P(None, ("gx", "gy", "gz")),
        P(),
        P(),
        P(),
        P(),
        P(),
        P(),
    )
    out_specs = P(("gx", "gy", "gz"), None)
    return jax.shard_map(
        on_device, mesh=mesh, in_specs=in_specs, out_specs=out_specs, check_vma=False
    )
```

```python
import math

import jax
import jax.numpy as jnp
from jax import lax
from jax.experimental import pallas as pl
from jax.experimental.pallas import tpu as pltpu
from jax.sharding import PartitionSpec as P

cutoff = 5.0
pair_scale = 0.25
basis_rows = 32
slot_group = 4
mebi = 1024 * 1024


def kernel_call(body, outs, operands, flops, limit, scratch=(), far=0):
    specs = [pl.BlockSpec(memory_space=pl.ANY)] * far
    specs += [pl.BlockSpec(memory_space=pltpu.VMEM)] * (len(operands) - far)
    moved = sum(math.prod(v.shape) * v.dtype.itemsize for v in (*operands, *outs))
    return pl.pallas_call(
        body,
        out_shape=tuple(outs),
        in_specs=specs,
        out_specs=(pl.BlockSpec(memory_space=pltpu.VMEM),) * len(outs),
        scratch_shapes=list(scratch),
        compiler_params=pltpu.CompilerParams(vmem_limit_bytes=limit * mebi),
        cost_estimate=pl.CostEstimate(flops=flops, bytes_accessed=moved, transcendentals=0),
    )(*operands)


def like(shape, dtype):
    return jax.ShapeDtypeStruct(shape, dtype)


def dot32(left, right):
    return jnp.dot(left, right, preferred_element_type=jnp.float32)


def picked(send, side, table):
    columns = jnp.concatenate([send] * 4, axis=0).T[:, side : side + 1]
    lanes = lax.broadcasted_iota(jnp.int32, (send.shape[1], table.shape[0]), 1)
    return dot32((columns == lanes).astype(jnp.bfloat16), table).astype(jnp.bfloat16)


def placed(send, below, above, rows):
    iota = lax.broadcasted_iota(jnp.int32, (rows, send.shape[1]), 0)
    low = dot32((iota == send[1:2]).astype(jnp.bfloat16), below)
    return low + dot32((iota == send[0:1]).astype(jnp.bfloat16), above)


def sides(axis):
    count = lax.axis_size(axis)
    here = lax.axis_index(axis).astype(jnp.int32)
    return lax.rem(here + count - 1, count), lax.rem(here + 1, count)


def unit_waves(coord, first, count):
    orders = (lax.broadcasted_iota(jnp.int32, (count, coord.shape[1]), 0) + first).astype(jnp.float32)
    turns = orders * coord
    angle = (2.0 * math.pi) * (turns - jnp.round(turns))
    return jnp.cos(angle), jnp.sin(angle)


def outer_waves(left, right):
    left_cos, left_sin = (v[:, None, :] for v in left)
    right_cos, right_sin = (v[None, :, :] for v in right)
    shape = (left_cos.shape[0] * right_cos.shape[1], left_cos.shape[2])
    cos_part = (left_cos * right_cos - left_sin * right_sin).reshape(shape)
    return cos_part, (left_sin * right_cos + left_cos * right_sin).reshape(shape)


def opening_body(*refs):
    far, (base_ref, blocks_ref, cos_ref, sin_ref), near, sems = refs[:6], refs[6:10], refs[10:16], refs[16]
    copies = [pltpu.make_async_copy(far[i], near[i], sems.at[i]) for i in range(6)]
    for copy in copies:
        copy.start()
    for copy in copies:
        copy.wait()
    feats_ref, one_ref, two_ref, send_ref, coords_ref, charge_ref = near
    feats = feats_ref[...]
    raw = dot32(feats, one_ref[...])
    hidden = (raw / (1.0 + jnp.exp(-raw))).astype(jnp.bfloat16)
    base = dot32(hidden, two_ref[...]).astype(jnp.bfloat16)
    base_ref[...] = base
    total, atoms = cos_ref.shape
    blocks, tall, width = blocks_ref.shape
    height = tall - send_ref.shape[1]
    lower, upper = sides("gx")
    blocks_ref[lower, height:] = picked(send_ref[...], 0, base)
    blocks_ref[upper, height:] = picked(send_ref[...], 1, base)

    firsts = total // 64
    coords = coords_ref[...]
    along_first = unit_waves(coords[0:1], -(firsts // 2), firsts)
    along_second = unit_waves(coords[1:2], -4, 8)
    along_third = unit_waves(coords[2:3], 1, 8)
    cos_part, sin_part = outer_waves(outer_waves(along_first, along_second), along_third)
    cos_table = cos_part.astype(jnp.bfloat16)
    sin_table = sin_part.astype(jnp.bfloat16)
    cos_ref[...] = cos_table
    sin_ref[...] = sin_table
    over_last = (((1,), (1,)), ((), ()))
    charge_t = lax.dot_general(charge_ref[...], feats, over_last, preferred_element_type=jnp.float32).astype(jnp.bfloat16)
    real = lax.dot_general(charge_t, cos_table, over_last, preferred_element_type=jnp.float32)
    imag = lax.dot_general(charge_t, sin_table, over_last, preferred_element_type=jnp.float32)
    both = jnp.concatenate([real, imag], axis=0).astype(blocks_ref.dtype)
    across = total // width
    for block in range(blocks):
        down, along = block // across * height, block % across * width
        blocks_ref[block, :height] = both[down : down + height, along : along + width]


def spread_body(
    dist_ref, nbr_ref, count_ref, base_ref, wide_ref, core_ref, blocks_ref, radial_ref, basis_ref
):
    slots, atoms = dist_ref.shape
    feat = base_ref.shape[1]
    core, half = core_ref.shape[0], blocks_ref.shape[1]
    distance = dist_ref[...]
    angle = (math.pi / cutoff) * distance
    turn = jnp.cos(angle)
    listed = lax.broadcasted_iota(jnp.int32, (slots, atoms), 0) < count_ref[...]
    fade = jnp.where(listed, 0.5 * (turn + 1.0), 0.0) / distance
    turn = turn + turn
    basis_ref[...] = jnp.zeros_like(basis_ref)
    before, now = jnp.zeros_like(angle), jnp.sin(angle)
    for order in range(20):
        term = now * fade
        for row in range(0, slots, 8):
            place = pl.ds(row * basis_rows + order, 8, stride=basis_rows)
            basis_ref[place, :] = term[row : row + 8]
        before, now = now, turn * now - before
    base = base_ref[...]
    iota = lax.broadcasted_iota(jnp.int32, (core + 2 * half, atoms), 0)
    group_rows = slot_group * basis_rows
    pickers, outward = [], []
    for group in range(slots // slot_group):
        block = basis_ref[group * group_rows : (group + 1) * group_rows, :].T.astype(jnp.bfloat16)
        wide = dot32(block, wide_ref[...]).astype(jnp.bfloat16)
        for offset in range(slot_group):
            slot = group * slot_group + offset
            radial = wide[:, offset * feat : (offset + 1) * feat]
            radial_ref[slot] = radial
            outward.append(radial * base)
            pickers.append((iota == nbr_ref[slot : slot + 1, :]).astype(jnp.bfloat16))
    total = dot32(jnp.concatenate(pickers, axis=1), jnp.concatenate(outward, axis=0))
    core_ref[...] = total[:core]
    lower, upper = sides("gz")
    blocks_ref[lower] = total[core : core + half].astype(jnp.bfloat16)
    blocks_ref[upper] = total[core + half :].astype(jnp.bfloat16)


def second_body(
    first_ref, third_ref, base_ref, core_ref, send_y_ref, send_z_ref,
    table_ref, keep_ref, low_ref, high_ref, copies_ref,
):
    height = copies_ref.shape[1]
    lower, upper = sides("gx")
    table = jnp.concatenate([base_ref[...], first_ref[lower, height:], first_ref[upper, height:]], axis=0)
    table_ref[...] = table
    total = jnp.sum(first_ref[:, :height].astype(jnp.float32), axis=0)
    copies_ref[...] = jnp.broadcast_to(total.astype(copies_ref.dtype)[None], copies_ref.shape)
    below, above = sides("gz")
    spread = core_ref[...] + placed(send_z_ref[...], third_ref[below], third_ref[above], core_ref.shape[0])
    keep, half = keep_ref.shape[0], send_y_ref.shape[1]
    keep_ref[...] = spread[:keep]
    low_ref[:half] = picked(send_y_ref[...], 0, table)
    high_ref[:half] = picked(send_y_ref[...], 1, table)
    low_ref[half:] = spread[keep : keep + half].astype(jnp.bfloat16)
    high_ref[half:] = spread[keep + half :].astype(jnp.bfloat16)


def third_body(
    below_ref, above_ref, table_ref, core_ref, send_y_ref, send_z_ref, longer_ref, keep_ref, low_ref, high_ref, blocks_ref
):
    half = send_y_ref.shape[1]
    table = jnp.concatenate([table_ref[...], below_ref[:half], above_ref[:half]], axis=0)
    longer_ref[...] = table
    lower, upper = sides("gz")
    blocks_ref[lower] = picked(send_z_ref[...], 0, table)
    blocks_ref[upper] = picked(send_z_ref[...], 1, table)
    spread = core_ref[...] + placed(send_y_ref[...], below_ref[half:], above_ref[half:], core_ref.shape[0])
    keep, rim = keep_ref.shape[0], low_ref.shape[0]
    keep_ref[...] = spread[:keep]
    low_ref[...] = spread[keep : keep + rim].astype(jnp.bfloat16)
    high_ref[...] = spread[keep + rim :].astype(jnp.bfloat16)


def factor_body(parts_ref, kernel_ref, low_ref, high_ref, blocks_ref, norm_factor):
    blocks, tall, width = blocks_ref.shape
    height = parts_ref.shape[1]
    across = kernel_ref.shape[1] // width
    here = lax.axis_index("gx").astype(jnp.int32)
    down, along = lax.div(here, across), lax.rem(here, across)
    weights = kernel_ref[:, pl.ds(pl.multiple_of(along * width, width), width)]
    weights = jnp.where(lax.rem(down, 2) == 0, weights[:height], weights[height:])
    total = jnp.sum(parts_ref[...].astype(jnp.float32), axis=0)
    factors = (total * weights * norm_factor).astype(blocks_ref.dtype)
    blocks_ref[:, :height] = jnp.broadcast_to(factors[None], (blocks, height, width))
    lower, upper = sides("gx")
    blocks_ref[lower, height:] = low_ref[...]
    blocks_ref[upper, height:] = high_ref[...]


def gather_body(nbr_ref, radial_ref, table_ref, third_ref, gathered_ref):
    slots, atoms = nbr_ref.shape
    lower, upper = sides("gz")
    table = jnp.concatenate([table_ref[...], third_ref[lower], third_ref[upper]], axis=0)
    lanes = lax.broadcasted_iota(jnp.int32, (atoms, table.shape[0]), 1)
    partner = nbr_ref[...].T
    total = jnp.zeros(gathered_ref.shape, jnp.float32)
    for slot in range(slots):
        picker = (partner[:, slot : slot + 1] == lanes).astype(jnp.bfloat16)
        total = total + dot32(picker, table) * radial_ref[slot].astype(jnp.float32)
    gathered_ref[...] = total


def update_body(first_ref, core_ref, send_ref, gathered_ref, cos_ref, sin_ref, ewald_ref, out_ref):
    blocks, tall, width = first_ref.shape
    height = tall - send_ref.shape[1]
    lower, upper = sides("gx")
    returned = core_ref[...] + placed(
        send_ref[...], first_ref[lower, height:], first_ref[upper, height:], core_ref.shape[0]
    )
    pair_update = (gathered_ref[...] + returned) * pair_scale
    total = cos_ref.shape[0]
    across = total // width
    lines = []
    for down in range(blocks // across):
        lines.append(jnp.concatenate([first_ref[down * across + i, :height] for i in range(across)], axis=1))
    real = dot32(jnp.concatenate(lines[: len(lines) // 2], axis=0), cos_ref[...])
    imag = dot32(jnp.concatenate(lines[len(lines) // 2 :], axis=0), sin_ref[...])
    field = ((real + imag) * (1.0 / math.sqrt(total))).T.astype(jnp.bfloat16)
    out_ref[...] = (pair_update + dot32(field, ewald_ref[...])).astype(out_ref.dtype)


def swap(low, high, axis):
    count = lax.axis_size(axis)
    forward = [(i, (i + 1) % count) for i in range(count)]
    backward = [(target, source) for source, target in forward]
    return lax.ppermute(high, axis, forward), lax.ppermute(low, axis, backward)


def exchange(blocks, axes):
    return lax.all_to_all(blocks, axes, split_axis=0, concat_axis=0)


def on_device(
    feats,
    coords,
    pair_dist,
    nbr_index,
    nbr_count,
    send_x,
    send_y,
    send_z,
    w_one,
    w_two,
    w_radial,
    w_charge,
    k_kernel,
    w_ewald,
):
    atoms, feat = feats.shape
    slots = pair_dist.shape[1]
    charges = w_charge.shape[1]
    total = k_kernel.shape[0]
    rim_x, rim_y, rim_z = send_x.shape[1], send_y.shape[1], send_z.shape[1]
    with_x = atoms + 2 * rim_x
    with_y = with_x + 2 * rim_y
    half, full = jnp.bfloat16, jnp.float32
    count_x, count_z = lax.axis_size("gx"), lax.axis_size("gz")
    count_yz = lax.axis_size("gy") * count_z
    height = 2 * charges * (total // 128) // count_x
    tall = height + rim_x

    far = (feats, w_one, w_two, send_x, coords, w_charge.T)
    base, blocks, cos_table, sin_table = kernel_call(
        opening_body,
        (
            like((atoms, feat), half), like((count_x, tall, feat), half),
            like((total, atoms), half), like((total, atoms), half),
        ),
        far, 10**8, 16,
        (*(pltpu.VMEM(v.shape, v.dtype) for v in far), pltpu.SemaphoreType.DMA((len(far),))), far=len(far),
    )
    first = exchange(blocks, "gx")

    padded = jnp.pad(w_radial, ((0, basis_rows - w_radial.shape[0]), (0, 0)))
    wide = jnp.concatenate(
        [jnp.pad(padded, ((0, 0), (i * feat, (slot_group - 1 - i) * feat))) for i in range(slot_group)], axis=0
    )
    core, blocks, radial = kernel_call(
        spread_body,
        (like((with_y, feat), full), like((count_z, rim_z, feat), half), like((slots, atoms, feat), half)),
        (pair_dist.T, nbr_index.T, nbr_count[None, :], base, wide), 6 * 10**9, 32,
        (pltpu.VMEM((slots * basis_rows, atoms), full),),
    )
    third = exchange(blocks, "gz")

    table, core, low, high, copies = kernel_call(
        second_body,
        (
            like((with_x, feat), half), like((with_x, feat), full), like((2 * rim_y, feat), half),
            like((2 * rim_y, feat), half), like((count_yz, height, feat), half),
        ),
        (first, third, base, core, send_y, send_z), 10**8, 8,
    )
    below, above = swap(low, high, "gy")
    parts = exchange(copies, ("gy", "gz"))
    table, core, low, high, blocks = kernel_call(
        third_body,
        (
            like((with_y, feat), half), like((atoms, feat), full), like((rim_x, feat), half),
            like((rim_x, feat), half), like((count_z, rim_z, feat), half),
        ),
        (below, above, table, core, send_y, send_z), 10**8, 8,
    )
    third = exchange(blocks, "gz")

    norm_factor = 1.0 / math.sqrt(atoms * count_x * count_yz)
    (blocks,) = kernel_call(
        lambda *refs: factor_body(*refs, norm_factor),
        (like((count_x, tall, feat), half),), (parts, k_kernel.T, low, high), 10**6, 8,
    )
    first = exchange(blocks, "gx")
    (gathered,) = kernel_call(
        gather_body, (like((atoms, feat), full),), (nbr_index.T, radial, table, third), 6 * 10**9, 32
    )
    (update,) = kernel_call(
        update_body, (like((atoms, feat), half),),
        (first, core, send_x, gathered, cos_table, sin_table, w_ewald), 10**8, 16,
    )
    return update


def solution(mesh):
    in_specs = (
        P(("gx", "gy", "gz"), None),
        P(None, ("gx", "gy", "gz")),
        P(("gx", "gy", "gz"), None),
        P(("gx", "gy", "gz"), None),
        P(("gx", "gy", "gz")),
        P(None, ("gx", "gy", "gz")),
        P(None, ("gx", "gy", "gz")),
        P(None, ("gx", "gy", "gz")),
        P(),
        P(),
        P(),
        P(),
        P(),
        P(),
    )
    out_specs = P(("gx", "gy", "gz"), None)
    return jax.shard_map(
        on_device, mesh=mesh, in_specs=in_specs, out_specs=out_specs, check_vma=False
    )
```

```python
import math

import jax
import jax.numpy as jnp
from jax import lax
from jax.experimental import pallas as pl
from jax.experimental.pallas import tpu as pltpu
from jax.sharding import PartitionSpec as P

cutoff = 5.0
pair_scale = 0.25
basis_rows = 32
slot_group = 4
mebi = 1024 * 1024


def kernel_call(body, outs, operands, flops, limit, scratch=(), far=0):
    specs = [pl.BlockSpec(memory_space=pltpu.HBM)] * far
    specs += [pl.BlockSpec(memory_space=pltpu.VMEM)] * (len(operands) - far)
    moved = sum(math.prod(v.shape) * v.dtype.itemsize for v in (*operands, *outs))
    return pl.pallas_call(
        body,
        out_shape=tuple(outs),
        in_specs=specs,
        out_specs=(pl.BlockSpec(memory_space=pltpu.VMEM),) * len(outs),
        scratch_shapes=list(scratch),
        compiler_params=pltpu.CompilerParams(vmem_limit_bytes=limit * mebi),
        cost_estimate=pl.CostEstimate(flops=flops, bytes_accessed=moved, transcendentals=0),
    )(*operands)


def like(shape, dtype):
    return jax.ShapeDtypeStruct(shape, dtype)


def dot32(left, right):
    return jnp.dot(left, right, preferred_element_type=jnp.float32)


def picked(send, side, table):
    columns = jnp.concatenate([send] * 4, axis=0).T[:, side : side + 1]
    lanes = lax.broadcasted_iota(jnp.int32, (send.shape[1], table.shape[0]), 1)
    return dot32((columns == lanes).astype(jnp.bfloat16), table).astype(jnp.bfloat16)


def placed(send, below, above, rows):
    iota = lax.broadcasted_iota(jnp.int32, (rows, send.shape[1]), 0)
    low = dot32((iota == send[1:2]).astype(jnp.bfloat16), below)
    return low + dot32((iota == send[0:1]).astype(jnp.bfloat16), above)


def fetched(far, near, sems):
    copies = [pltpu.make_async_copy(far[i], near[i], sems.at[i]) for i in range(len(far))]
    for copy in copies:
        copy.start()
    for copy in copies:
        copy.wait()
    return near


def landing(far):
    return (*(pltpu.VMEM(v.shape, v.dtype) for v in far), pltpu.SemaphoreType.DMA((len(far),)))


def sides(axis):
    count = lax.axis_size(axis)
    here = lax.axis_index(axis).astype(jnp.int32)
    return lax.rem(here + count - 1, count), lax.rem(here + 1, count)


def unit_waves(coord, first, count):
    orders = (lax.broadcasted_iota(jnp.int32, (count, coord.shape[1]), 0) + first).astype(jnp.float32)
    turns = orders * coord
    angle = (2.0 * math.pi) * (turns - jnp.round(turns))
    return jnp.cos(angle), jnp.sin(angle)


def outer_waves(left, right):
    left_cos, left_sin = (v[:, None, :] for v in left)
    right_cos, right_sin = (v[None, :, :] for v in right)
    shape = (left_cos.shape[0] * right_cos.shape[1], left_cos.shape[2])
    cos_part = (left_cos * right_cos - left_sin * right_sin).reshape(shape)
    return cos_part, (left_sin * right_cos + left_cos * right_sin).reshape(shape)


def opening_body(*refs):
    far, (base_ref, blocks_ref, cos_ref, sin_ref), near, sems = refs[:6], refs[6:10], refs[10:16], refs[16]
    feats_ref, one_ref, two_ref, send_ref, coords_ref, charge_ref = fetched(far, near, sems)
    feats = feats_ref[...]
    raw = dot32(feats, one_ref[...])
    hidden = (raw / (1.0 + jnp.exp(-raw))).astype(jnp.bfloat16)
    base = dot32(hidden, two_ref[...]).astype(jnp.bfloat16)
    base_ref[...] = base
    total, atoms = cos_ref.shape
    blocks, tall, width = blocks_ref.shape
    height = tall - send_ref.shape[1]
    lower, upper = sides("gx")
    blocks_ref[lower, height:] = picked(send_ref[...], 0, base)
    blocks_ref[upper, height:] = picked(send_ref[...], 1, base)

    firsts = total // 64
    coords = coords_ref[...]
    along_first = unit_waves(coords[0:1], -(firsts // 2), firsts)
    along_second = unit_waves(coords[1:2], -4, 8)
    along_third = unit_waves(coords[2:3], 1, 8)
    cos_part, sin_part = outer_waves(outer_waves(along_first, along_second), along_third)
    cos_table = cos_part.astype(jnp.bfloat16)
    sin_table = sin_part.astype(jnp.bfloat16)
    cos_ref[...] = cos_table
    sin_ref[...] = sin_table
    over_last = (((1,), (1,)), ((), ()))
    charge_t = lax.dot_general(charge_ref[...], feats, over_last, preferred_element_type=jnp.float32).astype(jnp.bfloat16)
    real = lax.dot_general(charge_t, cos_table, over_last, preferred_element_type=jnp.float32)
    imag = lax.dot_general(charge_t, sin_table, over_last, preferred_element_type=jnp.float32)
    both = jnp.concatenate([real, imag], axis=0).astype(blocks_ref.dtype)
    across = total // width
    for block in range(blocks):
        down, along = block // across * height, block % across * width
        blocks_ref[block, :height] = both[down : down + height, along : along + width]


def spread_body(*refs):
    far, (base_ref, core_ref, low_ref, high_ref, radial_ref, basis_ref) = refs[:4], refs[4:10]
    dist_ref, nbr_ref, count_ref, weight_ref = fetched(far, refs[10:14], refs[14])
    slots, atoms = dist_ref.shape
    feat = base_ref.shape[1]
    core, half = core_ref.shape[0], low_ref.shape[0]
    distance = dist_ref[...]
    angle = (math.pi / cutoff) * distance
    turn = jnp.cos(angle)
    listed = lax.broadcasted_iota(jnp.int32, (slots, atoms), 0) < count_ref[...]
    fade = jnp.where(listed, 0.5 * (turn + 1.0), 0.0) / distance
    turn = turn + turn
    basis_ref[...] = jnp.zeros_like(basis_ref)
    before, now = jnp.zeros_like(angle), jnp.sin(angle)
    for order in range(20):
        term = now * fade
        for row in range(0, slots, 8):
            place = pl.ds(row * basis_rows + order, 8, stride=basis_rows)
            basis_ref[place, :] = term[row : row + 8]
        before, now = now, turn * now - before
    base = base_ref[...]
    iota = lax.broadcasted_iota(jnp.int32, (core + 2 * half, atoms), 0)
    group_rows = slot_group * basis_rows
    shape = (group_rows, weight_ref.shape[0])
    down, along = (lax.broadcasted_iota(jnp.int32, shape, i) for i in range(2))
    wide = []
    for offset in range(slot_group):
        mover = (down == along + offset * basis_rows).astype(jnp.bfloat16)
        wide.append(dot32(mover, weight_ref[...]).astype(jnp.bfloat16))
    weights = jnp.concatenate(wide, axis=1)
    pickers, outward = [], []
    for group in range(slots // slot_group):
        block = basis_ref[group * group_rows : (group + 1) * group_rows, :].T.astype(jnp.bfloat16)
        wide = dot32(block, weights).astype(jnp.bfloat16)
        for offset in range(slot_group):
            slot = group * slot_group + offset
            radial = wide[:, offset * feat : (offset + 1) * feat]
            radial_ref[slot] = radial
            outward.append(radial * base)
            pickers.append((iota == nbr_ref[slot : slot + 1, :]).astype(jnp.bfloat16))
    total = dot32(jnp.concatenate(pickers, axis=1), jnp.concatenate(outward, axis=0))
    core_ref[...] = total[:core]
    low_ref[...] = total[core : core + half].astype(jnp.bfloat16)
    high_ref[...] = total[core + half :].astype(jnp.bfloat16)


def second_body(first_ref, base_ref, low_ref, high_ref, table_ref, blocks_ref):
    height = blocks_ref.shape[1] - low_ref.shape[0]
    lower, upper = sides("gx")
    table_ref[...] = jnp.concatenate(
        [base_ref[...], first_ref[lower, height:], first_ref[upper, height:]], axis=0
    )
    total = jnp.sum(first_ref[:, :height].astype(jnp.float32), axis=0).astype(blocks_ref.dtype)
    for peer in range(blocks_ref.shape[0]):
        blocks_ref[peer, :height] = total
    lower, upper = sides("gz")
    blocks_ref[lower, height:] = low_ref[...]
    blocks_ref[upper, height:] = high_ref[...]


def third_body(
    third_ref, table_ref, core_ref, send_y_ref, send_z_ref, keep_ref, low_ref, high_ref, share_ref
):
    height, half = share_ref.shape[0], send_y_ref.shape[1]
    share = jnp.sum(third_ref[:, :height].astype(jnp.float32), axis=0).astype(share_ref.dtype)
    share_ref[...] = share
    below, above = sides("gz")
    spread = core_ref[...] + placed(
        send_z_ref[...], third_ref[below, height:], third_ref[above, height:], core_ref.shape[0]
    )
    keep = keep_ref.shape[0]
    keep_ref[...] = spread[:keep]
    table = table_ref[...]
    for side, packet_ref in enumerate((low_ref, high_ref)):
        rows = slice(keep + side * half, keep + (side + 1) * half)
        packet_ref[:height] = share
        packet_ref[height : height + half] = picked(send_y_ref[...], side, table)
        packet_ref[height + half :] = spread[rows].astype(jnp.bfloat16)


def fourth_body(
    below_ref, above_ref, share_ref, across_ref, table_ref, core_ref, send_y_ref, send_z_ref, kernel_ref,
    longer_ref, keep_ref, low_ref, high_ref, blocks_ref, norm_factor,
):
    height, half = share_ref.shape[0], send_y_ref.shape[1]
    fresh, back = slice(height, height + half), slice(height + half, height + 2 * half)
    table = jnp.concatenate([table_ref[...], below_ref[fresh], above_ref[fresh]], axis=0)
    longer_ref[...] = table
    low_ref[...] = picked(send_z_ref[...], 0, table)
    high_ref[...] = picked(send_z_ref[...], 1, table)
    spread = core_ref[...] + placed(send_y_ref[...], below_ref[back], above_ref[back], core_ref.shape[0])
    keep = keep_ref.shape[0]
    keep_ref[...] = spread[:keep]

    blocks, tall, width = blocks_ref.shape
    rim = tall - height
    across = kernel_ref.shape[1] // width
    here = lax.axis_index("gx").astype(jnp.int32)
    down, along = lax.div(here, across), lax.rem(here, across)
    weights = kernel_ref[:, pl.ds(pl.multiple_of(along * width, width), width)]
    weights = jnp.where(lax.rem(down, 2) == 0, weights[:height], weights[height:])
    parts = (share_ref[...], across_ref[...], below_ref[:height], above_ref[:height])
    total = sum(part.astype(jnp.float32) for part in parts)
    factors = (total * weights * norm_factor).astype(blocks_ref.dtype)
    blocks_ref[:, :height] = jnp.broadcast_to(factors[None], (blocks, height, width))
    lower, upper = sides("gx")
    blocks_ref[lower, height:] = spread[keep : keep + rim].astype(jnp.bfloat16)
    blocks_ref[upper, height:] = spread[keep + rim :].astype(jnp.bfloat16)


def gather_body(nbr_ref, radial_ref, table_ref, below_ref, above_ref, gathered_ref):
    slots, atoms = nbr_ref.shape
    table = jnp.concatenate([table_ref[...], below_ref[...], above_ref[...]], axis=0)
    lanes = lax.broadcasted_iota(jnp.int32, (atoms, table.shape[0]), 1)
    partner = nbr_ref[...].T
    total = jnp.zeros(gathered_ref.shape, jnp.float32)
    for slot in range(slots):
        picker = (partner[:, slot : slot + 1] == lanes).astype(jnp.bfloat16)
        total = total + dot32(picker, table) * radial_ref[slot].astype(jnp.float32)
    gathered_ref[...] = total


def update_body(first_ref, core_ref, send_ref, gathered_ref, cos_ref, sin_ref, ewald_ref, out_ref):
    blocks, tall, width = first_ref.shape
    height = tall - send_ref.shape[1]
    lower, upper = sides("gx")
    returned = core_ref[...] + placed(
        send_ref[...], first_ref[lower, height:], first_ref[upper, height:], core_ref.shape[0]
    )
    pair_update = (gathered_ref[...] + returned) * pair_scale
    total = cos_ref.shape[0]
    across = total // width
    lines = []
    for down in range(blocks // across):
        lines.append(jnp.concatenate([first_ref[down * across + i, :height] for i in range(across)], axis=1))
    real = dot32(jnp.concatenate(lines[: len(lines) // 2], axis=0), cos_ref[...])
    imag = dot32(jnp.concatenate(lines[len(lines) // 2 :], axis=0), sin_ref[...])
    field = ((real + imag) * (1.0 / math.sqrt(total))).T.astype(jnp.bfloat16)
    out_ref[...] = (pair_update + dot32(field, ewald_ref[...])).astype(out_ref.dtype)


def swap(low, high, axis):
    count = lax.axis_size(axis)
    forward = [(i, (i + 1) % count) for i in range(count)]
    backward = [(target, source) for source, target in forward]
    return lax.ppermute(high, axis, forward), lax.ppermute(low, axis, backward)


def exchange(blocks, axes):
    return lax.all_to_all(blocks, axes, split_axis=0, concat_axis=0)


def on_device(
    feats,
    coords,
    pair_dist,
    nbr_index,
    nbr_count,
    send_x,
    send_y,
    send_z,
    w_one,
    w_two,
    w_radial,
    w_charge,
    k_kernel,
    w_ewald,
):
    atoms, feat = feats.shape
    slots = pair_dist.shape[1]
    charges = w_charge.shape[1]
    total = k_kernel.shape[0]
    rim_x, rim_y, rim_z = send_x.shape[1], send_y.shape[1], send_z.shape[1]
    with_x = atoms + 2 * rim_x
    with_y = with_x + 2 * rim_y
    half, full = jnp.bfloat16, jnp.float32
    count_x, count_y, count_z = (lax.axis_size(axis) for axis in ("gx", "gy", "gz"))
    height = 2 * charges * (total // 128) // count_x
    tall = height + rim_x

    far = (feats, w_one, w_two, send_x, coords, w_charge.T)
    base, blocks, cos_table, sin_table = kernel_call(
        opening_body,
        (
            like((atoms, feat), half), like((count_x, tall, feat), half),
            like((total, atoms), half), like((total, atoms), half),
        ),
        far, 10**8, 60, landing(far), far=len(far),
    )
    first = exchange(blocks, "gx")

    far = (pair_dist.T, nbr_index.T, nbr_count[None, :], w_radial)
    core, low, high, radial = kernel_call(
        spread_body,
        (
            like((with_y, feat), full), like((rim_z, feat), half), like((rim_z, feat), half),
            like((slots, atoms, feat), half),
        ),
        (*far, base), 6 * 10**9, 60, (pltpu.VMEM((slots * basis_rows, atoms), full), *landing(far)), far=len(far),
    )
    table, blocks = kernel_call(
        second_body,
        (like((with_x, feat), half), like((count_z, height + rim_z, feat), half)),
        (first, base, low, high), 10**8, 8,
    )
    third = exchange(blocks, "gz")
    core, low, high, share = kernel_call(
        third_body,
        (
            like((with_x, feat), full), like((height + 2 * rim_y, feat), half),
            like((height + 2 * rim_y, feat), half), like((height, feat), half),
        ),
        (third, table, core, send_y, send_z), 10**8, 8,
    )
    below, above = swap(low, high, "gy")
    across = lax.ppermute(share, "gy", [(i, (i + 2) % count_y) for i in range(count_y)])
    norm_factor = 1.0 / math.sqrt(atoms * count_x * count_y * count_z)
    table, core, low, high, blocks = kernel_call(
        lambda *refs: fourth_body(*refs, norm_factor),
        (
            like((with_y, feat), half), like((atoms, feat), full), like((rim_z, feat), half),
            like((rim_z, feat), half), like((count_x, tall, feat), half),
        ),
        (below, above, share, across, table, core, send_y, send_z, k_kernel.T), 10**8, 8,
    )
    below, above = swap(low, high, "gz")
    first = exchange(blocks, "gx")
    (gathered,) = kernel_call(
        gather_body, (like((atoms, feat), full),), (nbr_index.T, radial, table, below, above), 6 * 10**9, 32
    )
    (update,) = kernel_call(
        update_body, (like((atoms, feat), half),),
        (first, core, send_x, gathered, cos_table, sin_table, w_ewald), 10**8, 16,
    )
    return update


def solution(mesh):
    in_specs = (
        P(("gx", "gy", "gz"), None),
        P(None, ("gx", "gy", "gz")),
        P(("gx", "gy", "gz"), None),
        P(("gx", "gy", "gz"), None),
        P(("gx", "gy", "gz")),
        P(None, ("gx", "gy", "gz")),
        P(None, ("gx", "gy", "gz")),
        P(None, ("gx", "gy", "gz")),
        P(),
        P(),
        P(),
        P(),
        P(),
        P(),
    )
    out_specs = P(("gx", "gy", "gz"), None)
    return jax.shard_map(
        on_device, mesh=mesh, in_specs=in_specs, out_specs=out_specs, check_vma=False
    )
```

```python
import functools
import math

import jax
import jax.numpy as jnp
from jax import lax
from jax.experimental import pallas as pl
from jax.experimental.pallas import tpu as pltpu
from jax.sharding import PartitionSpec as P

cutoff = 5.0
pair_scale = 0.25
basis_rows = 32
slot_group = 4
mebi = 1024 * 1024


def kernel_call(body, outs, operands, flops, limit, scratch=(), far=0, moved=None):
    specs = [pl.BlockSpec(memory_space=pltpu.HBM)] * far
    specs += [pl.BlockSpec(memory_space=pltpu.VMEM)] * (len(operands) - far)
    if moved is None:
        moved = sum(math.prod(v.shape) * v.dtype.itemsize for v in (*operands, *outs))
    return pl.pallas_call(
        body,
        out_shape=tuple(outs),
        in_specs=specs,
        out_specs=(pl.BlockSpec(memory_space=pltpu.VMEM),) * len(outs),
        scratch_shapes=list(scratch),
        compiler_params=pltpu.CompilerParams(vmem_limit_bytes=limit * mebi),
        cost_estimate=pl.CostEstimate(flops=flops, bytes_accessed=moved, transcendentals=0),
    )(*operands)


def like(shape, dtype):
    return jax.ShapeDtypeStruct(shape, dtype)


def dot32(left, right):
    return jnp.dot(left, right, preferred_element_type=jnp.float32)


def picked(send, side, table):
    columns = jnp.concatenate([send] * 4, axis=0).T[:, side : side + 1]
    lanes = lax.broadcasted_iota(jnp.int32, (send.shape[1], table.shape[0]), 1)
    return dot32((columns == lanes).astype(jnp.bfloat16), table).astype(jnp.bfloat16)


def placed(send, below, above, rows):
    iota = lax.broadcasted_iota(jnp.int32, (rows, send.shape[1]), 0)
    low = dot32((iota == send[1:2]).astype(jnp.bfloat16), below)
    return low + dot32((iota == send[0:1]).astype(jnp.bfloat16), above)


def fetched(far, near, sems):
    copies = [pltpu.make_async_copy(far[i], near[i], sems.at[i]) for i in range(len(far))]
    for copy in copies:
        copy.start()
    for copy in copies:
        copy.wait()
    return near


def landing(far):
    return (*(pltpu.VMEM(v.shape, v.dtype) for v in far), pltpu.SemaphoreType.DMA((len(far),)))


def sides(axis):
    count = lax.axis_size(axis)
    here = lax.axis_index(axis).astype(jnp.int32)
    return lax.rem(here + count - 1, count), lax.rem(here + 1, count)


def unit_waves(coord, first, count):
    orders = (lax.broadcasted_iota(jnp.int32, (count, coord.shape[1]), 0) + first).astype(jnp.float32)
    turns = orders * coord
    angle = (2.0 * math.pi) * (turns - jnp.round(turns))
    return jnp.cos(angle), jnp.sin(angle)


def outer_waves(left, right):
    left_cos, left_sin = (v[:, None, :] for v in left)
    right_cos, right_sin = (v[None, :, :] for v in right)
    shape = (left_cos.shape[0] * right_cos.shape[1], left_cos.shape[2])
    cos_part = (left_cos * right_cos - left_sin * right_sin).reshape(shape)
    return cos_part, (left_sin * right_cos + left_cos * right_sin).reshape(shape)


def wave_tables(coords, total):
    firsts = total // 64
    along_first = unit_waves(coords[0:1], -(firsts // 2), firsts)
    along_second = unit_waves(coords[1:2], -4, 8)
    along_third = unit_waves(coords[2:3], 1, 8)
    cos_part, sin_part = outer_waves(outer_waves(along_first, along_second), along_third)
    return cos_part.astype(jnp.bfloat16), sin_part.astype(jnp.bfloat16)


def opening_body(total, *refs):
    far, (base_ref, blocks_ref) = refs[:6], refs[6:8]
    feats_ref, one_ref, two_ref, send_ref, coords_ref, charge_ref = fetched(far, refs[8:14], refs[14])
    feats = feats_ref[...]
    raw = dot32(feats, one_ref[...])
    hidden = (raw / (1.0 + jnp.exp(-raw))).astype(jnp.bfloat16)
    base = dot32(hidden, two_ref[...]).astype(jnp.bfloat16)
    base_ref[...] = base
    blocks, tall, width = blocks_ref.shape
    height = tall - send_ref.shape[1]
    for side, peer in enumerate(sides("gx")):
        blocks_ref[peer, height:] = picked(send_ref[...], side, base)
    cos_table, sin_table = wave_tables(coords_ref[...], total)
    over_last = (((1,), (1,)), ((), ()))
    charge_t = lax.dot_general(charge_ref[...], feats, over_last, preferred_element_type=jnp.float32).astype(jnp.bfloat16)
    real = lax.dot_general(charge_t, cos_table, over_last, preferred_element_type=jnp.float32)
    imag = lax.dot_general(charge_t, sin_table, over_last, preferred_element_type=jnp.float32)
    both = jnp.concatenate([real, imag], axis=0).astype(blocks_ref.dtype)
    across = total // width
    for block in range(blocks):
        down, along = block // across * height, block % across * width
        blocks_ref[block, :height] = both[down : down + height, along : along + width]


def spread_body(*refs):
    far, (base_ref, core_ref, rim_ref, cos_ref, sin_ref, radial_ref, basis_ref) = refs[:5], refs[5:12]
    dist_ref, nbr_ref, count_ref, weight_ref, coords_ref = fetched(far, refs[12:17], refs[17])
    slots, atoms = dist_ref.shape
    feat = base_ref.shape[1]
    core, rim = core_ref.shape[0], rim_ref.shape[0]
    distance = dist_ref[...]
    angle = (math.pi / cutoff) * distance
    turn = jnp.cos(angle)
    listed = lax.broadcasted_iota(jnp.int32, (slots, atoms), 0) < count_ref[...]
    fade = jnp.where(listed, 0.5 * (turn + 1.0), 0.0) / distance
    turn = turn + turn
    basis_ref[...] = jnp.zeros_like(basis_ref)
    before, now = jnp.zeros_like(angle), jnp.sin(angle)
    for order in range(20):
        term = now * fade
        for row in range(0, slots, 8):
            place = pl.ds(row * basis_rows + order, 8, stride=basis_rows)
            basis_ref[place, :] = term[row : row + 8]
        before, now = now, turn * now - before
    base = base_ref[...]
    iota = lax.broadcasted_iota(jnp.int32, (core + rim, atoms), 0)
    group_rows = slot_group * basis_rows
    shape = (group_rows, weight_ref.shape[0])
    down, along = (lax.broadcasted_iota(jnp.int32, shape, i) for i in range(2))
    wide = []
    for offset in range(slot_group):
        mover = (down == along + offset * basis_rows).astype(jnp.bfloat16)
        wide.append(dot32(mover, weight_ref[...]).astype(jnp.bfloat16))
    weights = jnp.concatenate(wide, axis=1)
    pickers, outward = [], []
    for group in range(slots // slot_group):
        block = basis_ref[group * group_rows : (group + 1) * group_rows, :].T.astype(jnp.bfloat16)
        wide = dot32(block, weights).astype(jnp.bfloat16)
        for offset in range(slot_group):
            slot = group * slot_group + offset
            radial = wide[:, offset * feat : (offset + 1) * feat]
            radial_ref[slot] = radial
            outward.append(radial * base)
            pickers.append((iota == nbr_ref[slot : slot + 1, :]).astype(jnp.bfloat16))
    total = dot32(jnp.concatenate(pickers, axis=1), jnp.concatenate(outward, axis=0))
    core_ref[...] = total[:core]
    rim_ref[...] = total[core:].astype(jnp.bfloat16)
    cos_ref[...], sin_ref[...] = wave_tables(coords_ref[...], cos_ref.shape[0])


def second_body(first_ref, rim_ref, blocks_ref):
    half = rim_ref.shape[0] // 2
    height = blocks_ref.shape[1] - half
    total = jnp.sum(first_ref[:, :height].astype(jnp.float32), axis=0).astype(blocks_ref.dtype)
    for peer in range(blocks_ref.shape[0]):
        blocks_ref[peer, :height] = total
    for side, peer in enumerate(sides("gz")):
        blocks_ref[peer, height:] = rim_ref[side * half : (side + 1) * half]


def pick_body(first_ref, base_ref, send_ref, table_ref, packets_ref):
    height = first_ref.shape[1] - (table_ref.shape[0] - base_ref.shape[0]) // 2
    lower, upper = sides("gx")
    table = jnp.concatenate([base_ref[...], first_ref[lower, height:], first_ref[upper, height:]], axis=0)
    table_ref[...] = table
    for side in range(2):
        packets_ref[side] = picked(send_ref[...], side, table)


def third_body(third_ref, packets_ref, core_ref, send_z_ref, keep_ref, low_ref, high_ref, share_ref):
    half = packets_ref.shape[1]
    height = low_ref.shape[0] - 2 * half
    share = jnp.sum(third_ref[:, :height].astype(jnp.float32), axis=0).astype(share_ref.dtype)
    share_ref[:height] = share
    below, above = sides("gz")
    spread = core_ref[...] + placed(
        send_z_ref[...], third_ref[below, height:], third_ref[above, height:], core_ref.shape[0]
    )
    keep = keep_ref.shape[0]
    keep_ref[...] = spread[:keep]
    for side, packet_ref in enumerate((low_ref, high_ref)):
        rows = slice(keep + side * half, keep + (side + 1) * half)
        packet_ref[:height] = share
        packet_ref[height : height + half] = packets_ref[side]
        packet_ref[height + half :] = spread[rows].astype(jnp.bfloat16)


def add_body(left_ref, right_ref, total_ref):
    height = total_ref.shape[0]
    total_ref[...] = left_ref[:height].astype(jnp.float32) + right_ref[:height].astype(jnp.float32)


def relay_body(above_ref, relay_ref):
    relay_ref[...] = above_ref[: relay_ref.shape[0]]


def fourth_body(
    below_ref, above_ref, share_ref, relay_ref, table_ref, core_ref, send_y_ref, send_z_ref, kernel_ref,
    gathered_ref, keep_ref, low_ref, high_ref, blocks_ref, norm_factor,
):
    height, half = share_ref.shape[0], send_y_ref.shape[1]
    fresh, back = slice(height, height + half), slice(height + half, height + 2 * half)
    table = jnp.concatenate([table_ref[...], below_ref[fresh], above_ref[fresh]], axis=0)
    low_ref[...] = picked(send_z_ref[...], 0, table)
    high_ref[...] = picked(send_z_ref[...], 1, table)
    spread = core_ref[...] + placed(send_y_ref[...], below_ref[back], above_ref[back], core_ref.shape[0])
    keep = keep_ref.shape[0]
    keep_ref[...] = spread[:keep]

    blocks, tall, width = blocks_ref.shape
    rim = tall - height
    across = kernel_ref.shape[1] // width
    here = lax.axis_index("gx").astype(jnp.int32)
    down, along = lax.div(here, across), lax.rem(here, across)
    weights = kernel_ref[:, pl.ds(pl.multiple_of(along * width, width), width)]
    weights = jnp.where(lax.rem(down, 2) == 0, weights[:height], weights[height:])
    parts = (share_ref[...], relay_ref[...], below_ref[:height], above_ref[:height])
    total = sum(part.astype(jnp.float32) for part in parts)
    factors = (total * weights * norm_factor).astype(blocks_ref.dtype)
    blocks_ref[:, :height] = jnp.broadcast_to(factors[None], (blocks, height, width))
    lower, upper = sides("gx")
    blocks_ref[lower, height:] = spread[keep : keep + rim].astype(jnp.bfloat16)
    blocks_ref[upper, height:] = spread[keep + rim :].astype(jnp.bfloat16)


def gather_rows(first_row, table, nbr_ref, radial_ref):
    slots, atoms = nbr_ref.shape
    lanes = lax.broadcasted_iota(jnp.int32, (atoms, table.shape[0]), 1) + first_row
    partner = nbr_ref[...].T
    total = jnp.zeros((atoms, table.shape[1]), jnp.float32)
    for slot in range(slots):
        picker = (partner[:, slot : slot + 1] == lanes).astype(jnp.bfloat16)
        total = total + dot32(picker, table) * radial_ref[slot].astype(jnp.float32)
    return total


def gather_first_body(nbr_ref, radial_ref, table_ref, order_ref, gathered_ref):
    gathered_ref[...] = gather_rows(0, table_ref[...], nbr_ref, radial_ref)


def gather_more_body(first_row, rows, nbr_ref, radial_ref, below_ref, above_ref, sofar_ref, gathered_ref):
    table = jnp.concatenate([below_ref[rows], above_ref[rows]], axis=0)
    gathered_ref[...] = sofar_ref[...] + gather_rows(first_row, table, nbr_ref, radial_ref)


def update_body(first_ref, core_ref, send_ref, gathered_ref, cos_ref, sin_ref, ewald_ref, out_ref):
    blocks, tall, width = first_ref.shape
    height = tall - send_ref.shape[1]
    lower, upper = sides("gx")
    returned = core_ref[...] + placed(
        send_ref[...], first_ref[lower, height:], first_ref[upper, height:], core_ref.shape[0]
    )
    pair_update = (gathered_ref[...] + returned) * pair_scale
    total = cos_ref.shape[0]
    across = total // width
    lines = []
    for down in range(blocks // across):
        lines.append(jnp.concatenate([first_ref[down * across + i, :height] for i in range(across)], axis=1))
    real = dot32(jnp.concatenate(lines[: len(lines) // 2], axis=0), cos_ref[...])
    imag = dot32(jnp.concatenate(lines[len(lines) // 2 :], axis=0), sin_ref[...])
    field = ((real + imag) * (1.0 / math.sqrt(total))).T.astype(jnp.bfloat16)
    out_ref[...] = (pair_update + dot32(field, ewald_ref[...])).astype(out_ref.dtype)


def swap(low, high, axis):
    count = lax.axis_size(axis)
    forward = [(i, (i + 1) % count) for i in range(count)]
    backward = [(target, source) for source, target in forward]
    return lax.ppermute(high, axis, forward), lax.ppermute(low, axis, backward)


def exchange(blocks, axes):
    return lax.all_to_all(blocks, axes, split_axis=0, concat_axis=0)


def on_device(
    feats,
    coords,
    pair_dist,
    nbr_index,
    nbr_count,
    send_x,
    send_y,
    send_z,
    w_one,
    w_two,
    w_radial,
    w_charge,
    k_kernel,
    w_ewald,
):
    atoms, feat = feats.shape
    slots = pair_dist.shape[1]
    charges = w_charge.shape[1]
    total = k_kernel.shape[0]
    rim_x, rim_y, rim_z = send_x.shape[1], send_y.shape[1], send_z.shape[1]
    with_x = atoms + 2 * rim_x
    with_y = with_x + 2 * rim_y
    half, full = jnp.bfloat16, jnp.float32
    count_x, count_y, count_z = (lax.axis_size(axis) for axis in ("gx", "gy", "gz"))
    height = 2 * charges * (total // 128) // count_x
    tall = height + rim_x

    far = (feats, w_one, w_two, send_x, coords, w_charge.T)
    base, blocks = kernel_call(
        functools.partial(opening_body, total),
        (like((atoms, feat), half), like((count_x, tall, feat), half)),
        far, 10**8, 60, landing(far), far=len(far),
    )
    first = exchange(blocks, "gx")

    far = (pair_dist.T, nbr_index.T, nbr_count[None, :], w_radial, coords)
    core, rim, cos_table, sin_table, radial = kernel_call(
        spread_body,
        (
            like((with_y, feat), full), like((2 * rim_z, feat), half), like((total, atoms), half),
            like((total, atoms), half), like((slots, atoms, feat), half),
        ),
        (*far, base), 6 * 10**9, 60, (pltpu.VMEM((slots * basis_rows, atoms), full), *landing(far)), far=len(far),
    )
    (blocks,) = kernel_call(
        second_body, (like((count_z, height + rim_z, feat), half),), (first, rim), 10**8, 8
    )
    third = exchange(blocks, "gz")
    table, packets = kernel_call(
        pick_body, (like((with_x, feat), half), like((2, rim_y, feat), half)), (first, base, send_y), 2 * 10**9, 8
    )
    core, low, high, share = kernel_call(
        third_body,
        (
            like((with_x, feat), full), like((height + 2 * rim_y, feat), half),
            like((height + 2 * rim_y, feat), half), like((224, feat), half),
        ),
        (third, packets, core, send_z), 10**8, 8,
    )
    early = lax.ppermute(share, "gy", [(2, 0)])
    below_y, above_y = swap(low, high, "gy")
    (partial,) = kernel_call(add_body, (like((height, feat), full),), (share, early), 10**11, 8)
    (gathered,) = kernel_call(
        gather_first_body, (like((atoms, feat), full),), (nbr_index.T, radial, table, partial), 10**3, 24, moved=10**3
    )
    (relay,) = kernel_call(
        relay_body, (like((height, feat), half),), (above_y,), 10**6, 8
    )
    relay = lax.ppermute(relay, "gy", [(0, 3), (3, 2), (2, 1)])
    norm_factor = 1.0 / math.sqrt(atoms * count_x * count_y * count_z)
    core, low, high, blocks = kernel_call(
        lambda *refs: fourth_body(*refs, norm_factor),
        (
            like((atoms, feat), full), like((rim_z, feat), half), like((rim_z, feat), half),
            like((count_x, tall, feat), half),
        ),
        (below_y, above_y, partial, relay, table, core, send_y, send_z, k_kernel.T, gathered), 10**8, 8,
    )
    below_z, above_z = swap(low, high, "gz")
    first = exchange(blocks, "gx")
    (gathered,) = kernel_call(
        functools.partial(gather_more_body, with_x, slice(height, height + rim_y)), (like((atoms, feat), full),),
        (nbr_index.T, radial, below_y, above_y, gathered), 2 * 10**9, 24,
    )
    (gathered,) = kernel_call(
        functools.partial(gather_more_body, with_y, slice(0, rim_z)), (like((atoms, feat), full),),
        (nbr_index.T, radial, below_z, above_z, gathered), 2 * 10**9, 24,
    )
    (update,) = kernel_call(
        update_body, (like((atoms, feat), half),),
        (first, core, send_x, gathered, cos_table, sin_table, w_ewald), 10**8, 16,
    )
    return update


def solution(mesh):
    in_specs = (
        P(("gx", "gy", "gz"), None),
        P(None, ("gx", "gy", "gz")),
        P(("gx", "gy", "gz"), None),
        P(("gx", "gy", "gz"), None),
        P(("gx", "gy", "gz")),
        P(None, ("gx", "gy", "gz")),
        P(None, ("gx", "gy", "gz")),
        P(None, ("gx", "gy", "gz")),
        P(),
        P(),
        P(),
        P(),
        P(),
        P(),
    )
    out_specs = P(("gx", "gy", "gz"), None)
    return jax.shard_map(
        on_device, mesh=mesh, in_specs=in_specs, out_specs=out_specs, check_vma=False
    )
```

```python
import functools
import math

import jax
import jax.numpy as jnp
from jax import lax
from jax.experimental import pallas as pl
from jax.experimental.pallas import tpu as pltpu
from jax.sharding import PartitionSpec as P

cutoff = 5.0
pair_scale = 0.25
basis_rows = 32
slot_group = 4
mebi = 1024 * 1024


def kernel_call(body, outs, operands, flops, limit, scratch=(), far=0, moved=None):
    specs = [pl.BlockSpec(memory_space=pltpu.HBM)] * far
    specs += [pl.BlockSpec(memory_space=pltpu.VMEM)] * (len(operands) - far)
    if moved is None:
        moved = sum(math.prod(v.shape) * v.dtype.itemsize for v in (*operands, *outs))
    return pl.pallas_call(
        body,
        out_shape=tuple(outs),
        in_specs=specs,
        out_specs=(pl.BlockSpec(memory_space=pltpu.VMEM),) * len(outs),
        scratch_shapes=list(scratch),
        compiler_params=pltpu.CompilerParams(vmem_limit_bytes=limit * mebi),
        cost_estimate=pl.CostEstimate(flops=flops, bytes_accessed=moved, transcendentals=0),
    )(*operands)


def like(shape, dtype):
    return jax.ShapeDtypeStruct(shape, dtype)


def dot32(left, right):
    return jnp.dot(left, right, preferred_element_type=jnp.float32)


def picked(send, side, table):
    columns = jnp.concatenate([send] * 4, axis=0).T[:, side : side + 1]
    lanes = lax.broadcasted_iota(jnp.int32, (send.shape[1], table.shape[0]), 1)
    return dot32((columns == lanes).astype(jnp.bfloat16), table).astype(jnp.bfloat16)


def placed(send, below, above, rows):
    iota = lax.broadcasted_iota(jnp.int32, (rows, send.shape[1]), 0)
    low = dot32((iota == send[1:2]).astype(jnp.bfloat16), below)
    return low + dot32((iota == send[0:1]).astype(jnp.bfloat16), above)


def fetched(far, near, sems):
    copies = [pltpu.make_async_copy(far[i], near[i], sems.at[i]) for i in range(len(far))]
    for copy in copies:
        copy.start()
    for copy in copies:
        copy.wait()
    return near


def landing(far):
    return (*(pltpu.VMEM(v.shape, v.dtype) for v in far), pltpu.SemaphoreType.DMA((len(far),)))


def sides(axis):
    count = lax.axis_size(axis)
    here = lax.axis_index(axis).astype(jnp.int32)
    return lax.rem(here + count - 1, count), lax.rem(here + 1, count)


def unit_waves(coord, first, count):
    orders = (lax.broadcasted_iota(jnp.int32, (count, coord.shape[1]), 0) + first).astype(jnp.float32)
    turns = orders * coord
    angle = (2.0 * math.pi) * (turns - jnp.round(turns))
    return jnp.cos(angle), jnp.sin(angle)


def outer_waves(left, right):
    left_cos, left_sin = (v[:, None, :] for v in left)
    right_cos, right_sin = (v[None, :, :] for v in right)
    shape = (left_cos.shape[0] * right_cos.shape[1], left_cos.shape[2])
    cos_part = (left_cos * right_cos - left_sin * right_sin).reshape(shape)
    return cos_part, (left_sin * right_cos + left_cos * right_sin).reshape(shape)


def wave_tables(coords, total):
    firsts = total // 64
    along_first = unit_waves(coords[0:1], -(firsts // 2), firsts)
    along_second = unit_waves(coords[1:2], -4, 8)
    along_third = unit_waves(coords[2:3], 1, 8)
    cos_part, sin_part = outer_waves(outer_waves(along_first, along_second), along_third)
    return cos_part.astype(jnp.bfloat16), sin_part.astype(jnp.bfloat16)


def opening_body(total, *refs):
    far, (base_ref, blocks_ref) = refs[:6], refs[6:8]
    feats_ref, one_ref, two_ref, send_ref, coords_ref, charge_ref = fetched(far, refs[8:14], refs[14])
    feats = feats_ref[...]
    raw = dot32(feats, one_ref[...])
    hidden = (raw / (1.0 + jnp.exp(-raw))).astype(jnp.bfloat16)
    base = dot32(hidden, two_ref[...]).astype(jnp.bfloat16)
    base_ref[...] = base
    blocks, tall, width = blocks_ref.shape
    height = tall - send_ref.shape[1]
    for side, peer in enumerate(sides("gx")):
        blocks_ref[peer, height:] = picked(send_ref[...], side, base)
    cos_table, sin_table = wave_tables(coords_ref[...], total)
    over_last = (((1,), (1,)), ((), ()))
    charge_t = lax.dot_general(charge_ref[...], feats, over_last, preferred_element_type=jnp.float32).astype(jnp.bfloat16)
    real = lax.dot_general(charge_t, cos_table, over_last, preferred_element_type=jnp.float32)
    imag = lax.dot_general(charge_t, sin_table, over_last, preferred_element_type=jnp.float32)
    both = jnp.concatenate([real, imag], axis=0).astype(blocks_ref.dtype)
    across = total // width
    for block in range(blocks):
        down, along = block // across * height, block % across * width
        blocks_ref[block, :height] = both[down : down + height, along : along + width]


def spread_body(*refs):
    far, (base_ref, core_ref, rim_ref, cos_ref, sin_ref, radial_ref, basis_ref) = refs[:5], refs[5:12]
    dist_ref, nbr_ref, count_ref, weight_ref, coords_ref = fetched(far, refs[12:17], refs[17])
    slots, atoms = dist_ref.shape
    feat = base_ref.shape[1]
    core, rim = core_ref.shape[0], rim_ref.shape[0]
    distance = dist_ref[...]
    angle = (math.pi / cutoff) * distance
    turn = jnp.cos(angle)
    listed = lax.broadcasted_iota(jnp.int32, (slots, atoms), 0) < count_ref[...]
    fade = jnp.where(listed, 0.5 * (turn + 1.0), 0.0) / distance
    turn = turn + turn
    basis_ref[...] = jnp.zeros_like(basis_ref)
    before, now = jnp.zeros_like(angle), jnp.sin(angle)
    for order in range(20):
        term = now * fade
        for row in range(0, slots, 8):
            place = pl.ds(row * basis_rows + order, 8, stride=basis_rows)
            basis_ref[place, :] = term[row : row + 8]
        before, now = now, turn * now - before
    base = base_ref[...]
    iota = lax.broadcasted_iota(jnp.int32, (core + rim, atoms), 0)
    group_rows = slot_group * basis_rows
    shape = (group_rows, weight_ref.shape[0])
    down, along = (lax.broadcasted_iota(jnp.int32, shape, i) for i in range(2))
    wide = []
    for offset in range(slot_group):
        mover = (down == along + offset * basis_rows).astype(jnp.bfloat16)
        wide.append(dot32(mover, weight_ref[...]).astype(jnp.bfloat16))
    weights = jnp.concatenate(wide, axis=1)
    pickers, outward = [], []
    for group in range(slots // slot_group):
        block = basis_ref[group * group_rows : (group + 1) * group_rows, :].T.astype(jnp.bfloat16)
        wide = dot32(block, weights).astype(jnp.bfloat16)
        for offset in range(slot_group):
            slot = group * slot_group + offset
            radial = wide[:, offset * feat : (offset + 1) * feat]
            radial_ref[slot] = radial
            outward.append(radial * base)
            pickers.append((iota == nbr_ref[slot : slot + 1, :]).astype(jnp.bfloat16))
    total = dot32(jnp.concatenate(pickers, axis=1), jnp.concatenate(outward, axis=0))
    core_ref[...] = total[:core]
    rim_ref[...] = total[core:].astype(jnp.bfloat16)
    cos_ref[...], sin_ref[...] = wave_tables(coords_ref[...], cos_ref.shape[0])


def second_body(first_ref, rim_ref, blocks_ref):
    half = rim_ref.shape[0] // 2
    height = blocks_ref.shape[1] - half
    total = jnp.sum(first_ref[:, :height].astype(jnp.float32), axis=0).astype(blocks_ref.dtype)
    for peer in range(blocks_ref.shape[0]):
        blocks_ref[peer, :height] = total
    for side, peer in enumerate(sides("gz")):
        blocks_ref[peer, height:] = rim_ref[side * half : (side + 1) * half]


def pick_body(first_ref, base_ref, send_ref, table_ref, packets_ref):
    height = first_ref.shape[1] - (table_ref.shape[0] - base_ref.shape[0]) // 2
    lower, upper = sides("gx")
    table = jnp.concatenate([base_ref[...], first_ref[lower, height:], first_ref[upper, height:]], axis=0)
    table_ref[...] = table
    for side in range(2):
        packets_ref[side] = picked(send_ref[...], side, table)


def third_body(third_ref, packets_ref, core_ref, send_z_ref, keep_ref, low_ref, high_ref, share_ref):
    half = packets_ref.shape[1]
    height = low_ref.shape[0] - 2 * half
    share = jnp.sum(third_ref[:, :height].astype(jnp.float32), axis=0).astype(share_ref.dtype)
    share_ref[...] = share
    below, above = sides("gz")
    spread = core_ref[...] + placed(
        send_z_ref[...], third_ref[below, height:], third_ref[above, height:], core_ref.shape[0]
    )
    keep = keep_ref.shape[0]
    keep_ref[...] = spread[:keep]
    for side, packet_ref in enumerate((low_ref, high_ref)):
        rows = slice(keep + side * half, keep + (side + 1) * half)
        packet_ref[:height] = share
        packet_ref[height : height + half] = packets_ref[side]
        packet_ref[height + half :] = spread[rows].astype(jnp.bfloat16)


def relay_body(above_ref, relay_ref):
    relay_ref[...] = above_ref[: relay_ref.shape[0]]


def fourth_body(
    below_ref, above_ref, share_ref, relay_ref, table_ref, core_ref, send_y_ref, send_z_ref, kernel_ref,
    gathered_ref, keep_ref, low_ref, high_ref, blocks_ref, norm_factor,
):
    height, half = share_ref.shape[0], send_y_ref.shape[1]
    fresh, back = slice(height, height + half), slice(height + half, height + 2 * half)
    table = jnp.concatenate([table_ref[...], below_ref[fresh], above_ref[fresh]], axis=0)
    low_ref[...] = picked(send_z_ref[...], 0, table)
    high_ref[...] = picked(send_z_ref[...], 1, table)
    spread = core_ref[...] + placed(send_y_ref[...], below_ref[back], above_ref[back], core_ref.shape[0])
    keep = keep_ref.shape[0]
    keep_ref[...] = spread[:keep]

    blocks, tall, width = blocks_ref.shape
    rim = tall - height
    across = kernel_ref.shape[1] // width
    here = lax.axis_index("gx").astype(jnp.int32)
    down, along = lax.div(here, across), lax.rem(here, across)
    weights = kernel_ref[:, pl.ds(pl.multiple_of(along * width, width), width)]
    weights = jnp.where(lax.rem(down, 2) == 0, weights[:height], weights[height:])
    parts = (share_ref[...], relay_ref[...], below_ref[:height], above_ref[:height])
    total = sum(part.astype(jnp.float32) for part in parts)
    factors = (total * weights * norm_factor).astype(blocks_ref.dtype)
    blocks_ref[:, :height] = jnp.broadcast_to(factors[None], (blocks, height, width))
    lower, upper = sides("gx")
    blocks_ref[lower, height:] = spread[keep : keep + rim].astype(jnp.bfloat16)
    blocks_ref[upper, height:] = spread[keep + rim :].astype(jnp.bfloat16)


def gather_rows(first_row, table, nbr_ref, radial_ref):
    slots, atoms = nbr_ref.shape
    lanes = lax.broadcasted_iota(jnp.int32, (atoms, table.shape[0]), 1) + first_row
    partner = nbr_ref[...].T
    total = jnp.zeros((atoms, table.shape[1]), jnp.float32)
    for slot in range(slots):
        picker = (partner[:, slot : slot + 1] == lanes).astype(jnp.bfloat16)
        total = total + dot32(picker, table) * radial_ref[slot].astype(jnp.float32)
    return total


def gather_first_body(nbr_ref, radial_ref, table_ref, gathered_ref):
    gathered_ref[...] = gather_rows(0, table_ref[...], nbr_ref, radial_ref)


def gather_more_body(first_row, rows, nbr_ref, radial_ref, below_ref, above_ref, sofar_ref, gathered_ref):
    table = jnp.concatenate([below_ref[rows], above_ref[rows]], axis=0)
    gathered_ref[...] = sofar_ref[...] + gather_rows(first_row, table, nbr_ref, radial_ref)


def update_body(first_ref, core_ref, send_ref, gathered_ref, cos_ref, sin_ref, ewald_ref, out_ref):
    blocks, tall, width = first_ref.shape
    height = tall - send_ref.shape[1]
    lower, upper = sides("gx")
    returned = core_ref[...] + placed(
        send_ref[...], first_ref[lower, height:], first_ref[upper, height:], core_ref.shape[0]
    )
    pair_update = (gathered_ref[...] + returned) * pair_scale
    total = cos_ref.shape[0]
    across = total // width
    lines = []
    for down in range(blocks // across):
        lines.append(jnp.concatenate([first_ref[down * across + i, :height] for i in range(across)], axis=1))
    real = dot32(jnp.concatenate(lines[: len(lines) // 2], axis=0), cos_ref[...])
    imag = dot32(jnp.concatenate(lines[len(lines) // 2 :], axis=0), sin_ref[...])
    field = ((real + imag) * (1.0 / math.sqrt(total))).T.astype(jnp.bfloat16)
    out_ref[...] = (pair_update + dot32(field, ewald_ref[...])).astype(out_ref.dtype)


def swap(low, high, axis):
    count = lax.axis_size(axis)
    forward = [(i, (i + 1) % count) for i in range(count)]
    backward = [(target, source) for source, target in forward]
    return lax.ppermute(high, axis, forward), lax.ppermute(low, axis, backward)


def exchange(blocks, axes):
    return lax.all_to_all(blocks, axes, split_axis=0, concat_axis=0)


def on_device(
    feats,
    coords,
    pair_dist,
    nbr_index,
    nbr_count,
    send_x,
    send_y,
    send_z,
    w_one,
    w_two,
    w_radial,
    w_charge,
    k_kernel,
    w_ewald,
):
    atoms, feat = feats.shape
    slots = pair_dist.shape[1]
    charges = w_charge.shape[1]
    total = k_kernel.shape[0]
    rim_x, rim_y, rim_z = send_x.shape[1], send_y.shape[1], send_z.shape[1]
    with_x = atoms + 2 * rim_x
    with_y = with_x + 2 * rim_y
    half, full = jnp.bfloat16, jnp.float32
    count_x, count_y, count_z = (lax.axis_size(axis) for axis in ("gx", "gy", "gz"))
    height = 2 * charges * (total // 128) // count_x
    tall = height + rim_x

    far = (feats, w_one, w_two, send_x, coords, w_charge.T)
    base, blocks = kernel_call(
        functools.partial(opening_body, total),
        (like((atoms, feat), half), like((count_x, tall, feat), half)),
        far, 10**8, 60, landing(far), far=len(far),
    )
    first = exchange(blocks, "gx")

    far = (pair_dist.T, nbr_index.T, nbr_count[None, :], w_radial, coords)
    core, rim, cos_table, sin_table, radial = kernel_call(
        spread_body,
        (
            like((with_y, feat), full), like((2 * rim_z, feat), half), like((total, atoms), half),
            like((total, atoms), half), like((slots, atoms, feat), half),
        ),
        (*far, base), 6 * 10**9, 60, (pltpu.VMEM((slots * basis_rows, atoms), full), *landing(far)), far=len(far),
    )
    (blocks,) = kernel_call(
        second_body, (like((count_z, height + rim_z, feat), half),), (first, rim), 10**8, 8
    )
    third = exchange(blocks, "gz")
    table, packets = kernel_call(
        pick_body, (like((with_x, feat), half), like((2, rim_y, feat), half)), (first, base, send_y), 2 * 10**9, 8
    )
    core, low, high, share = kernel_call(
        third_body,
        (
            like((with_x, feat), full), like((height + 2 * rim_y, feat), half),
            like((height + 2 * rim_y, feat), half), like((height, feat), half),
        ),
        (third, packets, core, send_z), 10**8, 8,
    )
    below_y, above_y = swap(low, high, "gy")
    (gathered,) = kernel_call(
        gather_first_body, (like((atoms, feat), full),), (nbr_index.T, radial, table), 10**3, 24, moved=10**3
    )
    (relay,) = kernel_call(
        relay_body, (like((height, feat), half),), (below_y,), 10**6, 8
    )
    relay = lax.ppermute(relay, "gy", [(i, (i + 1) % count_y) for i in range(count_y)])
    norm_factor = 1.0 / math.sqrt(atoms * count_x * count_y * count_z)
    core, low, high, blocks = kernel_call(
        lambda *refs: fourth_body(*refs, norm_factor),
        (
            like((atoms, feat), full), like((rim_z, feat), half), like((rim_z, feat), half),
            like((count_x, tall, feat), half),
        ),
        (below_y, above_y, share, relay, table, core, send_y, send_z, k_kernel.T, gathered), 10**8, 8,
    )
    below_z, above_z = swap(low, high, "gz")
    first = exchange(blocks, "gx")
    (gathered,) = kernel_call(
        functools.partial(gather_more_body, with_x, slice(height, height + rim_y)), (like((atoms, feat), full),),
        (nbr_index.T, radial, below_y, above_y, gathered), 2 * 10**9, 24,
    )
    (gathered,) = kernel_call(
        functools.partial(gather_more_body, with_y, slice(0, rim_z)), (like((atoms, feat), full),),
        (nbr_index.T, radial, below_z, above_z, gathered), 2 * 10**9, 24,
    )
    (update,) = kernel_call(
        update_body, (like((atoms, feat), half),),
        (first, core, send_x, gathered, cos_table, sin_table, w_ewald), 10**8, 16,
    )
    return update


def solution(mesh):
    in_specs = (
        P(("gx", "gy", "gz"), None),
        P(None, ("gx", "gy", "gz")),
        P(("gx", "gy", "gz"), None),
        P(("gx", "gy", "gz"), None),
        P(("gx", "gy", "gz")),
        P(None, ("gx", "gy", "gz")),
        P(None, ("gx", "gy", "gz")),
        P(None, ("gx", "gy", "gz")),
        P(),
        P(),
        P(),
        P(),
        P(),
        P(),
    )
    out_specs = P(("gx", "gy", "gz"), None)
    return jax.shard_map(
        on_device, mesh=mesh, in_specs=in_specs, out_specs=out_specs, check_vma=False
    )
```

```python
import functools
import math

import jax
import jax.numpy as jnp
from jax import lax
from jax.experimental import pallas as pl
from jax.experimental.pallas import tpu as pltpu
from jax.sharding import PartitionSpec as P

cutoff = 5.0
pair_scale = 0.25
basis_rows = 32
slot_group = 4
mebi = 1024 * 1024


def kernel_call(body, outs, operands, flops, limit, scratch=(), far=0, moved=None):
    specs = [pl.BlockSpec(memory_space=pltpu.HBM)] * far
    specs += [pl.BlockSpec(memory_space=pltpu.VMEM)] * (len(operands) - far)
    if moved is None:
        moved = sum(math.prod(v.shape) * v.dtype.itemsize for v in (*operands, *outs))
    return pl.pallas_call(
        body,
        out_shape=tuple(outs),
        in_specs=specs,
        out_specs=(pl.BlockSpec(memory_space=pltpu.VMEM),) * len(outs),
        scratch_shapes=list(scratch),
        compiler_params=pltpu.CompilerParams(vmem_limit_bytes=limit * mebi),
        cost_estimate=pl.CostEstimate(flops=flops, bytes_accessed=moved, transcendentals=0),
    )(*operands)


def like(shape, dtype):
    return jax.ShapeDtypeStruct(shape, dtype)


def dot32(left, right):
    return jnp.dot(left, right, preferred_element_type=jnp.float32)


def picked(send, side, table):
    columns = jnp.concatenate([send] * 4, axis=0).T[:, side : side + 1]
    lanes = lax.broadcasted_iota(jnp.int32, (send.shape[1], table.shape[0]), 1)
    return dot32((columns == lanes).astype(jnp.bfloat16), table).astype(jnp.bfloat16)


def placed(send, below, above, rows):
    iota = lax.broadcasted_iota(jnp.int32, (rows, send.shape[1]), 0)
    low = dot32((iota == send[1:2]).astype(jnp.bfloat16), below)
    return low + dot32((iota == send[0:1]).astype(jnp.bfloat16), above)


def fetched(far, near, sems):
    copies = [pltpu.make_async_copy(far[i], near[i], sems.at[i]) for i in range(len(far))]
    for copy in copies:
        copy.start()
    for copy in copies:
        copy.wait()
    return near


def landing(far):
    return (*(pltpu.VMEM(v.shape, v.dtype) for v in far), pltpu.SemaphoreType.DMA((len(far),)))


def sides(axis):
    count = lax.axis_size(axis)
    here = lax.axis_index(axis).astype(jnp.int32)
    return lax.rem(here + count - 1, count), lax.rem(here + 1, count)


def unit_waves(coord, first, count):
    orders = (lax.broadcasted_iota(jnp.int32, (count, coord.shape[1]), 0) + first).astype(jnp.float32)
    turns = orders * coord
    angle = (2.0 * math.pi) * (turns - jnp.round(turns))
    return jnp.cos(angle), jnp.sin(angle)


def outer_waves(left, right):
    left_cos, left_sin = (v[:, None, :] for v in left)
    right_cos, right_sin = (v[None, :, :] for v in right)
    shape = (left_cos.shape[0] * right_cos.shape[1], left_cos.shape[2])
    cos_part = (left_cos * right_cos - left_sin * right_sin).reshape(shape)
    return cos_part, (left_sin * right_cos + left_cos * right_sin).reshape(shape)


def wave_tables(coords, total):
    firsts = total // 64
    along_first = unit_waves(coords[0:1], -(firsts // 2), firsts)
    along_second = unit_waves(coords[1:2], -4, 8)
    along_third = unit_waves(coords[2:3], 1, 8)
    cos_part, sin_part = outer_waves(outer_waves(along_first, along_second), along_third)
    return cos_part.astype(jnp.bfloat16), sin_part.astype(jnp.bfloat16)


def opening_body(total, *refs):
    far, (base_ref, blocks_ref) = refs[:6], refs[6:8]
    feats_ref, one_ref, two_ref, send_ref, coords_ref, charge_ref = fetched(far, refs[8:14], refs[14])
    feats = feats_ref[...]
    raw = dot32(feats, one_ref[...])
    hidden = (raw / (1.0 + jnp.exp(-raw))).astype(jnp.bfloat16)
    base = dot32(hidden, two_ref[...]).astype(jnp.bfloat16)
    base_ref[...] = base
    blocks, tall, width = blocks_ref.shape
    height = tall - send_ref.shape[1]
    for side, peer in enumerate(sides("gx")):
        blocks_ref[peer, height:] = picked(send_ref[...], side, base)
    cos_table, sin_table = wave_tables(coords_ref[...], total)
    over_last = (((1,), (1,)), ((), ()))
    charge_t = lax.dot_general(charge_ref[...], feats, over_last, preferred_element_type=jnp.float32).astype(jnp.bfloat16)
    real = lax.dot_general(charge_t, cos_table, over_last, preferred_element_type=jnp.float32)
    imag = lax.dot_general(charge_t, sin_table, over_last, preferred_element_type=jnp.float32)
    both = jnp.concatenate([real, imag], axis=0).astype(blocks_ref.dtype)
    across = total // width
    for block in range(blocks):
        down, along = block // across * height, block % across * width
        blocks_ref[block, :height] = both[down : down + height, along : along + width]


def spread_body(*refs):
    far, (base_ref, core_ref, rim_ref, cos_ref, sin_ref, radial_ref, basis_ref) = refs[:5], refs[5:12]
    dist_ref, nbr_ref, count_ref, weight_ref, coords_ref = fetched(far, refs[12:17], refs[17])
    slots, atoms = dist_ref.shape
    feat = base_ref.shape[1]
    core, rim = core_ref.shape[0], rim_ref.shape[0]
    distance = dist_ref[...]
    angle = (math.pi / cutoff) * distance
    turn = jnp.cos(angle)
    listed = lax.broadcasted_iota(jnp.int32, (slots, atoms), 0) < count_ref[...]
    fade = jnp.where(listed, 0.5 * (turn + 1.0), 0.0) / distance
    turn = turn + turn
    basis_ref[...] = jnp.zeros_like(basis_ref)
    before, now = jnp.zeros_like(angle), jnp.sin(angle)
    for order in range(20):
        term = now * fade
        for row in range(0, slots, 8):
            place = pl.ds(row * basis_rows + order, 8, stride=basis_rows)
            basis_ref[place, :] = term[row : row + 8]
        before, now = now, turn * now - before
    base = base_ref[...]
    iota = lax.broadcasted_iota(jnp.int32, (core + rim, atoms), 0)
    group_rows = slot_group * basis_rows
    shape = (group_rows, weight_ref.shape[0])
    down, along = (lax.broadcasted_iota(jnp.int32, shape, i) for i in range(2))
    wide = []
    for offset in range(slot_group):
        mover = (down == along + offset * basis_rows).astype(jnp.bfloat16)
        wide.append(dot32(mover, weight_ref[...]).astype(jnp.bfloat16))
    weights = jnp.concatenate(wide, axis=1)
    pickers, outward = [], []
    for group in range(slots // slot_group):
        block = basis_ref[group * group_rows : (group + 1) * group_rows, :].T.astype(jnp.bfloat16)
        wide = dot32(block, weights).astype(jnp.bfloat16)
        for offset in range(slot_group):
            slot = group * slot_group + offset
            radial = wide[:, offset * feat : (offset + 1) * feat]
            radial_ref[slot] = radial
            outward.append(radial * base)
            pickers.append((iota == nbr_ref[slot : slot + 1, :]).astype(jnp.bfloat16))
    total = dot32(jnp.concatenate(pickers, axis=1), jnp.concatenate(outward, axis=0))
    core_ref[...] = total[:core]
    rim_ref[...] = total[core:].astype(jnp.bfloat16)
    cos_ref[...], sin_ref[...] = wave_tables(coords_ref[...], cos_ref.shape[0])


def stage_body(source_ref, staged_ref):
    staged_ref[...] = source_ref[...]


def second_body(first_ref, rim_ref, blocks_ref):
    half = rim_ref.shape[0] // 2
    height = blocks_ref.shape[1] - half
    total = jnp.sum(first_ref[:, :height].astype(jnp.float32), axis=0).astype(blocks_ref.dtype)
    for peer in range(blocks_ref.shape[0]):
        blocks_ref[peer, :height] = total
    for side, peer in enumerate(sides("gz")):
        blocks_ref[peer, height:] = rim_ref[side * half : (side + 1) * half]


def pick_body(first_ref, base_ref, send_ref, table_ref, packets_ref):
    height = first_ref.shape[1] - (table_ref.shape[0] - base_ref.shape[0]) // 2
    lower, upper = sides("gx")
    table = jnp.concatenate([base_ref[...], first_ref[lower, height:], first_ref[upper, height:]], axis=0)
    table_ref[...] = table
    for side in range(2):
        packets_ref[side] = picked(send_ref[...], side, table)


def third_body(third_ref, packets_ref, core_ref, send_z_ref, keep_ref, low_ref, high_ref, share_ref):
    half = packets_ref.shape[1]
    height = low_ref.shape[0] - 2 * half
    share = jnp.sum(third_ref[:, :height].astype(jnp.float32), axis=0).astype(share_ref.dtype)
    share_ref[...] = share
    below, above = sides("gz")
    spread = core_ref[...] + placed(
        send_z_ref[...], third_ref[below, height:], third_ref[above, height:], core_ref.shape[0]
    )
    keep = keep_ref.shape[0]
    keep_ref[...] = spread[:keep]
    for side, packet_ref in enumerate((low_ref, high_ref)):
        rows = slice(keep + side * half, keep + (side + 1) * half)
        packet_ref[:height] = share
        packet_ref[height : height + half] = packets_ref[side]
        packet_ref[height + half :] = spread[rows].astype(jnp.bfloat16)


def relay_body(above_ref, relay_ref):
    relay_ref[...] = above_ref[: relay_ref.shape[0]]


def rim_body(fresh, below_ref, above_ref, table_ref, send_ref, order_ref, low_ref, high_ref):
    table = jnp.concatenate([table_ref[...], below_ref[fresh], above_ref[fresh]], axis=0)
    low_ref[...] = picked(send_ref[...], 0, table)
    high_ref[...] = picked(send_ref[...], 1, table)


def fourth_body(
    below_ref, above_ref, share_ref, relay_ref, core_ref, send_y_ref, kernel_ref,
    gathered_ref, keep_ref, blocks_ref, norm_factor,
):
    height, half = share_ref.shape[0], send_y_ref.shape[1]
    back = slice(height + half, height + 2 * half)
    spread = core_ref[...] + placed(send_y_ref[...], below_ref[back], above_ref[back], core_ref.shape[0])
    keep = keep_ref.shape[0]
    keep_ref[...] = spread[:keep]

    blocks, tall, width = blocks_ref.shape
    rim = tall - height
    across = kernel_ref.shape[1] // width
    here = lax.axis_index("gx").astype(jnp.int32)
    down, along = lax.div(here, across), lax.rem(here, across)
    weights = kernel_ref[:, pl.ds(pl.multiple_of(along * width, width), width)]
    weights = jnp.where(lax.rem(down, 2) == 0, weights[:height], weights[height:])
    parts = (share_ref[...], relay_ref[...], below_ref[:height], above_ref[:height])
    total = sum(part.astype(jnp.float32) for part in parts)
    factors = (total * weights * norm_factor).astype(blocks_ref.dtype)
    blocks_ref[:, :height] = jnp.broadcast_to(factors[None], (blocks, height, width))
    lower, upper = sides("gx")
    blocks_ref[lower, height:] = spread[keep : keep + rim].astype(jnp.bfloat16)
    blocks_ref[upper, height:] = spread[keep + rim :].astype(jnp.bfloat16)


def gather_rows(first_row, table, nbr_ref, radial_ref):
    slots, atoms = nbr_ref.shape
    lanes = lax.broadcasted_iota(jnp.int32, (atoms, table.shape[0]), 1) + first_row
    partner = nbr_ref[...].T
    total = jnp.zeros((atoms, table.shape[1]), jnp.float32)
    for slot in range(slots):
        picker = (partner[:, slot : slot + 1] == lanes).astype(jnp.bfloat16)
        total = total + dot32(picker, table) * radial_ref[slot].astype(jnp.float32)
    return total


def gather_first_body(nbr_ref, radial_ref, table_ref, gathered_ref):
    gathered_ref[...] = gather_rows(0, table_ref[...], nbr_ref, radial_ref)


def gather_more_body(first_row, rows, nbr_ref, radial_ref, below_ref, above_ref, sofar_ref, gathered_ref):
    table = jnp.concatenate([below_ref[rows], above_ref[rows]], axis=0)
    gathered_ref[...] = sofar_ref[...] + gather_rows(first_row, table, nbr_ref, radial_ref)


def update_body(first_ref, core_ref, send_ref, gathered_ref, cos_ref, sin_ref, ewald_ref, out_ref):
    blocks, tall, width = first_ref.shape
    height = tall - send_ref.shape[1]
    lower, upper = sides("gx")
    returned = core_ref[...] + placed(
        send_ref[...], first_ref[lower, height:], first_ref[upper, height:], core_ref.shape[0]
    )
    pair_update = (gathered_ref[...] + returned) * pair_scale
    total = cos_ref.shape[0]
    across = total // width
    lines = []
    for down in range(blocks // across):
        lines.append(jnp.concatenate([first_ref[down * across + i, :height] for i in range(across)], axis=1))
    real = dot32(jnp.concatenate(lines[: len(lines) // 2], axis=0), cos_ref[...])
    imag = dot32(jnp.concatenate(lines[len(lines) // 2 :], axis=0), sin_ref[...])
    field = ((real + imag) * (1.0 / math.sqrt(total))).T.astype(jnp.bfloat16)
    out_ref[...] = (pair_update + dot32(field, ewald_ref[...])).astype(out_ref.dtype)


def swap(low, high, axis):
    count = lax.axis_size(axis)
    forward = [(i, (i + 1) % count) for i in range(count)]
    backward = [(target, source) for source, target in forward]
    return lax.ppermute(high, axis, forward), lax.ppermute(low, axis, backward)


def exchange(blocks, axes):
    return lax.all_to_all(blocks, axes, split_axis=0, concat_axis=0)


def on_device(
    feats,
    coords,
    pair_dist,
    nbr_index,
    nbr_count,
    send_x,
    send_y,
    send_z,
    w_one,
    w_two,
    w_radial,
    w_charge,
    k_kernel,
    w_ewald,
):
    atoms, feat = feats.shape
    slots = pair_dist.shape[1]
    charges = w_charge.shape[1]
    total = k_kernel.shape[0]
    rim_x, rim_y, rim_z = send_x.shape[1], send_y.shape[1], send_z.shape[1]
    with_x = atoms + 2 * rim_x
    with_y = with_x + 2 * rim_y
    half, full = jnp.bfloat16, jnp.float32
    count_x, count_y, count_z = (lax.axis_size(axis) for axis in ("gx", "gy", "gz"))
    height = 2 * charges * (total // 128) // count_x
    tall = height + rim_x

    far = (feats, w_one, w_two, send_x, coords, w_charge.T)
    base, blocks = kernel_call(
        functools.partial(opening_body, total),
        (like((atoms, feat), half), like((count_x, tall, feat), half)),
        far, 10**8, 60, landing(far), far=len(far),
    )
    first = exchange(blocks, "gx")

    far = (pair_dist.T, nbr_index.T, nbr_count[None, :], w_radial, coords)
    core, rim, cos_table, sin_table, radial = kernel_call(
        spread_body,
        (
            like((with_y, feat), full), like((2 * rim_z, feat), half), like((total, atoms), half),
            like((total, atoms), half), like((slots, atoms, feat), half),
        ),
        (*far, base), 6 * 10**9, 60, (pltpu.VMEM((slots * basis_rows, atoms), full), *landing(far)), far=len(far),
    )
    (rim,) = kernel_call(stage_body, (like(rim.shape, half),), (rim,), 10**6, 8)
    (blocks,) = kernel_call(
        second_body, (like((count_z, height + rim_z, feat), half),), (first, rim), 10**8, 8
    )
    third = exchange(blocks, "gz")
    table, packets = kernel_call(
        pick_body, (like((with_x, feat), half), like((2, rim_y, feat), half)), (first, base, send_y), 2 * 10**9, 8
    )
    core, low, high, share = kernel_call(
        third_body,
        (
            like((with_x, feat), full), like((height + 2 * rim_y, feat), half),
            like((height + 2 * rim_y, feat), half), like((height, feat), half),
        ),
        (third, packets, core, send_z), 10**8, 8,
    )
    below_y, above_y = swap(low, high, "gy")
    (gathered,) = kernel_call(
        gather_first_body, (like((atoms, feat), full),), (nbr_index.T, radial, table), 10**3, 24, moved=10**3
    )
    (relay,) = kernel_call(
        relay_body, (like((height, feat), half),), (below_y,), 10**6, 8
    )
    relay = lax.ppermute(relay, "gy", [(i, (i + 1) % count_y) for i in range(count_y)])
    norm_factor = 1.0 / math.sqrt(atoms * count_x * count_y * count_z)
    core, blocks = kernel_call(
        lambda *refs: fourth_body(*refs, norm_factor),
        (
            like((atoms, feat), full), like((count_x, tall, feat), half),
        ),
        (below_y, above_y, share, relay, core, send_y, k_kernel.T, gathered), 10**8, 8,
    )
    low, high = kernel_call(
        functools.partial(rim_body, slice(height, height + rim_y)), (like((rim_z, feat), half),) * 2,
        (below_y, above_y, table, send_z, core), 10**8, 8
    )
    below_z, above_z = swap(low, high, "gz")
    first = exchange(blocks, "gx")
    (gathered,) = kernel_call(
        functools.partial(gather_more_body, with_x, slice(height, height + rim_y)), (like((atoms, feat), full),),
        (nbr_index.T, radial, below_y, above_y, gathered), 2 * 10**9, 24,
    )
    (gathered,) = kernel_call(
        functools.partial(gather_more_body, with_y, slice(0, rim_z)), (like((atoms, feat), full),),
        (nbr_index.T, radial, below_z, above_z, gathered), 2 * 10**9, 24,
    )
    (update,) = kernel_call(
        update_body, (like((atoms, feat), half),),
        (first, core, send_x, gathered, cos_table, sin_table, w_ewald), 10**8, 16,
    )
    return update


def solution(mesh):
    in_specs = (
        P(("gx", "gy", "gz"), None),
        P(None, ("gx", "gy", "gz")),
        P(("gx", "gy", "gz"), None),
        P(("gx", "gy", "gz"), None),
        P(("gx", "gy", "gz")),
        P(None, ("gx", "gy", "gz")),
        P(None, ("gx", "gy", "gz")),
        P(None, ("gx", "gy", "gz")),
        P(),
        P(),
        P(),
        P(),
        P(),
        P(),
    )
    out_specs = P(("gx", "gy", "gz"), None)
    return jax.shard_map(
        on_device, mesh=mesh, in_specs=in_specs, out_specs=out_specs, check_vma=False
    )
```

```python
import functools
import math

import jax
import jax.numpy as jnp
from jax import lax
from jax.experimental import pallas as pl
from jax.experimental.pallas import tpu as pltpu
from jax.sharding import PartitionSpec as P

cutoff = 5.0
pair_scale = 0.25
basis_rows = 32
slot_group = 4
mebi = 1024 * 1024


def kernel_call(body, outs, operands, flops, limit, scratch=(), far=0, moved=None):
    specs = [pl.BlockSpec(memory_space=pltpu.HBM)] * far
    specs += [pl.BlockSpec(memory_space=pltpu.VMEM)] * (len(operands) - far)
    if moved is None:
        moved = sum(math.prod(v.shape) * v.dtype.itemsize for v in (*operands, *outs))
    return pl.pallas_call(
        body,
        out_shape=tuple(outs),
        in_specs=specs,
        out_specs=(pl.BlockSpec(memory_space=pltpu.VMEM),) * len(outs),
        scratch_shapes=list(scratch),
        compiler_params=pltpu.CompilerParams(vmem_limit_bytes=limit * mebi),
        cost_estimate=pl.CostEstimate(flops=flops, bytes_accessed=moved, transcendentals=0),
    )(*operands)


def like(shape, dtype):
    return jax.ShapeDtypeStruct(shape, dtype)


def dot32(left, right):
    return jnp.dot(left, right, preferred_element_type=jnp.float32)


def picked(send, side, table):
    columns = jnp.concatenate([send] * 4, axis=0).T[:, side : side + 1]
    lanes = lax.broadcasted_iota(jnp.int32, (send.shape[1], table.shape[0]), 1)
    return dot32((columns == lanes).astype(jnp.bfloat16), table).astype(jnp.bfloat16)


def placed(send, below, above, rows):
    iota = lax.broadcasted_iota(jnp.int32, (rows, send.shape[1]), 0)
    low = dot32((iota == send[1:2]).astype(jnp.bfloat16), below)
    return low + dot32((iota == send[0:1]).astype(jnp.bfloat16), above)


def fetched(far, near, sems):
    copies = [pltpu.make_async_copy(far[i], near[i], sems.at[i]) for i in range(len(far))]
    for copy in copies:
        copy.start()
    for copy in copies:
        copy.wait()
    return near


def landing(far):
    return (*(pltpu.VMEM(v.shape, v.dtype) for v in far), pltpu.SemaphoreType.DMA((len(far),)))


def sides(axis):
    count = lax.axis_size(axis)
    here = lax.axis_index(axis).astype(jnp.int32)
    return lax.rem(here + count - 1, count), lax.rem(here + 1, count)


def unit_waves(coord, first, count):
    orders = (lax.broadcasted_iota(jnp.int32, (count, coord.shape[1]), 0) + first).astype(jnp.float32)
    turns = orders * coord
    angle = (2.0 * math.pi) * (turns - jnp.round(turns))
    return jnp.cos(angle), jnp.sin(angle)


def outer_waves(left, right):
    left_cos, left_sin = (v[:, None, :] for v in left)
    right_cos, right_sin = (v[None, :, :] for v in right)
    shape = (left_cos.shape[0] * right_cos.shape[1], left_cos.shape[2])
    cos_part = (left_cos * right_cos - left_sin * right_sin).reshape(shape)
    return cos_part, (left_sin * right_cos + left_cos * right_sin).reshape(shape)


def wave_tables(coords, total):
    firsts = total // 64
    along_first = unit_waves(coords[0:1], -(firsts // 2), firsts)
    along_second = unit_waves(coords[1:2], -4, 8)
    along_third = unit_waves(coords[2:3], 1, 8)
    cos_part, sin_part = outer_waves(outer_waves(along_first, along_second), along_third)
    return cos_part.astype(jnp.bfloat16), sin_part.astype(jnp.bfloat16)


def opening_body(total, *refs):
    far, (base_ref, blocks_ref) = refs[:6], refs[6:8]
    feats_ref, one_ref, two_ref, send_ref, coords_ref, charge_ref = fetched(far, refs[8:14], refs[14])
    feats = feats_ref[...]
    raw = dot32(feats, one_ref[...])
    hidden = (raw / (1.0 + jnp.exp(-raw))).astype(jnp.bfloat16)
    base = dot32(hidden, two_ref[...]).astype(jnp.bfloat16)
    base_ref[...] = base
    blocks, tall, width = blocks_ref.shape
    height = tall - send_ref.shape[1]
    for side, peer in enumerate(sides("gx")):
        blocks_ref[peer, height:] = picked(send_ref[...], side, base)
    cos_table, sin_table = wave_tables(coords_ref[...], total)
    over_last = (((1,), (1,)), ((), ()))
    charge_t = lax.dot_general(charge_ref[...], feats, over_last, preferred_element_type=jnp.float32).astype(jnp.bfloat16)
    real = lax.dot_general(charge_t, cos_table, over_last, preferred_element_type=jnp.float32)
    imag = lax.dot_general(charge_t, sin_table, over_last, preferred_element_type=jnp.float32)
    both = jnp.concatenate([real, imag], axis=0).astype(blocks_ref.dtype)
    across = total // width
    for block in range(blocks):
        down, along = block // across * height, block % across * width
        blocks_ref[block, :height] = both[down : down + height, along : along + width]


def spread_body(*refs):
    far, (base_ref, core_ref, rim_ref, cos_ref, sin_ref, radial_ref, basis_ref) = refs[:5], refs[5:12]
    dist_ref, nbr_ref, count_ref, weight_ref, coords_ref = fetched(far, refs[12:17], refs[17])
    slots, atoms = dist_ref.shape
    feat = base_ref.shape[1]
    core, rim = core_ref.shape[0], rim_ref.shape[0]
    distance = dist_ref[...]
    angle = (math.pi / cutoff) * distance
    turn = jnp.cos(angle)
    listed = lax.broadcasted_iota(jnp.int32, (slots, atoms), 0) < count_ref[...]
    fade = jnp.where(listed, 0.5 * (turn + 1.0), 0.0) / distance
    turn = turn + turn
    basis_ref[...] = jnp.zeros_like(basis_ref)
    before, now = jnp.zeros_like(angle), jnp.sin(angle)
    for order in range(20):
        term = now * fade
        for row in range(0, slots, 8):
            place = pl.ds(row * basis_rows + order, 8, stride=basis_rows)
            basis_ref[place, :] = term[row : row + 8]
        before, now = now, turn * now - before
    base = base_ref[...]
    iota = lax.broadcasted_iota(jnp.int32, (core + rim, atoms), 0)
    group_rows = slot_group * basis_rows
    shape = (group_rows, weight_ref.shape[0])
    down, along = (lax.broadcasted_iota(jnp.int32, shape, i) for i in range(2))
    wide = []
    for offset in range(slot_group):
        mover = (down == along + offset * basis_rows).astype(jnp.bfloat16)
        wide.append(dot32(mover, weight_ref[...]).astype(jnp.bfloat16))
    weights = jnp.concatenate(wide, axis=1)
    pickers, outward = [], []
    for group in range(slots // slot_group):
        block = basis_ref[group * group_rows : (group + 1) * group_rows, :].T.astype(jnp.bfloat16)
        wide = dot32(block, weights).astype(jnp.bfloat16)
        for offset in range(slot_group):
            slot = group * slot_group + offset
            radial = wide[:, offset * feat : (offset + 1) * feat]
            radial_ref[slot] = radial
            outward.append(radial * base)
            pickers.append((iota == nbr_ref[slot : slot + 1, :]).astype(jnp.bfloat16))
    total = dot32(jnp.concatenate(pickers, axis=1), jnp.concatenate(outward, axis=0))
    core_ref[...] = total[:core]
    rim_ref[...] = total[core:].astype(jnp.bfloat16)
    cos_ref[...], sin_ref[...] = wave_tables(coords_ref[...], cos_ref.shape[0])


def stage_body(source_ref, staged_ref):
    staged_ref[...] = source_ref[...]


def second_body(first_ref, rim_ref, blocks_ref):
    half = rim_ref.shape[0] // 2
    height = blocks_ref.shape[1] - half
    total = jnp.sum(first_ref[:, :height].astype(jnp.float32), axis=0).astype(blocks_ref.dtype)
    for peer in range(blocks_ref.shape[0]):
        blocks_ref[peer, :height] = total
    for side, peer in enumerate(sides("gz")):
        blocks_ref[peer, height:] = rim_ref[side * half : (side + 1) * half]


def pick_body(first_ref, base_ref, send_ref, table_ref, packets_ref):
    height = first_ref.shape[1] - (table_ref.shape[0] - base_ref.shape[0]) // 2
    lower, upper = sides("gx")
    table = jnp.concatenate([base_ref[...], first_ref[lower, height:], first_ref[upper, height:]], axis=0)
    table_ref[...] = table
    for side in range(2):
        packets_ref[side] = picked(send_ref[...], side, table)


def third_body(third_ref, packets_ref, core_ref, send_z_ref, gathered_ref, keep_ref, low_ref, high_ref, share_ref):
    half = packets_ref.shape[1]
    height = low_ref.shape[0] - 2 * half
    share = jnp.sum(third_ref[:, :height].astype(jnp.float32), axis=0).astype(share_ref.dtype)
    share_ref[...] = share
    below, above = sides("gz")
    spread = core_ref[...] + placed(
        send_z_ref[...], third_ref[below, height:], third_ref[above, height:], core_ref.shape[0]
    )
    keep = keep_ref.shape[0]
    keep_ref[...] = spread[:keep]
    for side, packet_ref in enumerate((low_ref, high_ref)):
        rows = slice(keep + side * half, keep + (side + 1) * half)
        packet_ref[:height] = share
        packet_ref[height : height + half] = packets_ref[side]
        packet_ref[height + half :] = spread[rows].astype(jnp.bfloat16)


def relay_body(above_ref, relay_ref):
    relay_ref[...] = above_ref[: relay_ref.shape[0]]


def rim_body(fresh, below_ref, above_ref, table_ref, send_ref, order_ref, low_ref, high_ref):
    table = jnp.concatenate([table_ref[...], below_ref[fresh], above_ref[fresh]], axis=0)
    low_ref[...] = picked(send_ref[...], 0, table)
    high_ref[...] = picked(send_ref[...], 1, table)


def fourth_body(
    below_ref, above_ref, share_ref, relay_ref, core_ref, send_y_ref, kernel_ref,
    keep_ref, blocks_ref, norm_factor,
):
    height, half = share_ref.shape[0], send_y_ref.shape[1]
    back = slice(height + half, height + 2 * half)
    spread = core_ref[...] + placed(send_y_ref[...], below_ref[back], above_ref[back], core_ref.shape[0])
    keep = keep_ref.shape[0]
    keep_ref[...] = spread[:keep]

    blocks, tall, width = blocks_ref.shape
    rim = tall - height
    across = kernel_ref.shape[1] // width
    here = lax.axis_index("gx").astype(jnp.int32)
    down, along = lax.div(here, across), lax.rem(here, across)
    weights = kernel_ref[:, pl.ds(pl.multiple_of(along * width, width), width)]
    weights = jnp.where(lax.rem(down, 2) == 0, weights[:height], weights[height:])
    parts = (share_ref[...], relay_ref[...], below_ref[:height], above_ref[:height])
    total = sum(part.astype(jnp.float32) for part in parts)
    factors = (total * weights * norm_factor).astype(blocks_ref.dtype)
    blocks_ref[:, :height] = jnp.broadcast_to(factors[None], (blocks, height, width))
    lower, upper = sides("gx")
    blocks_ref[lower, height:] = spread[keep : keep + rim].astype(jnp.bfloat16)
    blocks_ref[upper, height:] = spread[keep + rim :].astype(jnp.bfloat16)


def gather_rows(first_row, table, nbr_ref, radial_ref):
    slots, atoms = nbr_ref.shape
    lanes = lax.broadcasted_iota(jnp.int32, (atoms, table.shape[0]), 1) + first_row
    partner = nbr_ref[...].T
    total = jnp.zeros((atoms, table.shape[1]), jnp.float32)
    for slot in range(slots):
        picker = (partner[:, slot : slot + 1] == lanes).astype(jnp.bfloat16)
        total = total + dot32(picker, table) * radial_ref[slot].astype(jnp.float32)
    return total


def gather_first_body(nbr_ref, radial_ref, table_ref, gathered_ref):
    gathered_ref[...] = gather_rows(0, table_ref[...], nbr_ref, radial_ref)


def gather_more_body(first_row, rows, nbr_ref, radial_ref, below_ref, above_ref, sofar_ref, gathered_ref):
    table = jnp.concatenate([below_ref[rows], above_ref[rows]], axis=0)
    gathered_ref[...] = sofar_ref[...] + gather_rows(first_row, table, nbr_ref, radial_ref)


def update_body(first_ref, core_ref, send_ref, gathered_ref, cos_ref, sin_ref, ewald_ref, out_ref):
    blocks, tall, width = first_ref.shape
    height = tall - send_ref.shape[1]
    lower, upper = sides("gx")
    returned = core_ref[...] + placed(
        send_ref[...], first_ref[lower, height:], first_ref[upper, height:], core_ref.shape[0]
    )
    pair_update = (gathered_ref[...] + returned) * pair_scale
    total = cos_ref.shape[0]
    across = total // width
    lines = []
    for down in range(blocks // across):
        lines.append(jnp.concatenate([first_ref[down * across + i, :height] for i in range(across)], axis=1))
    real = dot32(jnp.concatenate(lines[: len(lines) // 2], axis=0), cos_ref[...])
    imag = dot32(jnp.concatenate(lines[len(lines) // 2 :], axis=0), sin_ref[...])
    field = ((real + imag) * (1.0 / math.sqrt(total))).T.astype(jnp.bfloat16)
    out_ref[...] = (pair_update + dot32(field, ewald_ref[...])).astype(out_ref.dtype)


def swap(low, high, axis):
    count = lax.axis_size(axis)
    forward = [(i, (i + 1) % count) for i in range(count)]
    backward = [(target, source) for source, target in forward]
    return lax.ppermute(high, axis, forward), lax.ppermute(low, axis, backward)


def exchange(blocks, axes):
    return lax.all_to_all(blocks, axes, split_axis=0, concat_axis=0)


def on_device(
    feats,
    coords,
    pair_dist,
    nbr_index,
    nbr_count,
    send_x,
    send_y,
    send_z,
    w_one,
    w_two,
    w_radial,
    w_charge,
    k_kernel,
    w_ewald,
):
    atoms, feat = feats.shape
    slots = pair_dist.shape[1]
    charges = w_charge.shape[1]
    total = k_kernel.shape[0]
    rim_x, rim_y, rim_z = send_x.shape[1], send_y.shape[1], send_z.shape[1]
    with_x = atoms + 2 * rim_x
    with_y = with_x + 2 * rim_y
    half, full = jnp.bfloat16, jnp.float32
    count_x, count_y, count_z = (lax.axis_size(axis) for axis in ("gx", "gy", "gz"))
    height = 2 * charges * (total // 128) // count_x
    tall = height + rim_x

    far = (feats, w_one, w_two, send_x, coords, w_charge.T)
    base, blocks = kernel_call(
        functools.partial(opening_body, total),
        (like((atoms, feat), half), like((count_x, tall, feat), half)),
        far, 10**8, 60, landing(far), far=len(far),
    )
    first = exchange(blocks, "gx")

    far = (pair_dist.T, nbr_index.T, nbr_count[None, :], w_radial, coords)
    core, rim, cos_table, sin_table, radial = kernel_call(
        spread_body,
        (
            like((with_y, feat), full), like((2 * rim_z, feat), half), like((total, atoms), half),
            like((total, atoms), half), like((slots, atoms, feat), half),
        ),
        (*far, base), 6 * 10**9, 60, (pltpu.VMEM((slots * basis_rows, atoms), full), *landing(far)), far=len(far),
    )
    (rim,) = kernel_call(stage_body, (like(rim.shape, half),), (rim,), 10**6, 8)
    (blocks,) = kernel_call(
        second_body, (like((count_z, height + rim_z, feat), half),), (first, rim), 10**8, 8
    )
    third = exchange(blocks, "gz")
    table, packets = kernel_call(
        pick_body, (like((with_x, feat), half), like((2, rim_y, feat), half)), (first, base, send_y), 2 * 10**9, 8
    )
    (gathered,) = kernel_call(
        gather_first_body, (like((atoms, feat), full),), (nbr_index.T, radial, table), 10**3, 24, moved=10**3
    )
    core, low, high, share = kernel_call(
        third_body,
        (
            like((with_x, feat), full), like((height + 2 * rim_y, feat), half),
            like((height + 2 * rim_y, feat), half), like((height, feat), half),
        ),
        (third, packets, core, send_z, gathered), 10**8, 8,
    )
    below_y, above_y = swap(low, high, "gy")
    (relay,) = kernel_call(
        relay_body, (like((height, feat), half),), (below_y,), 10**6, 8
    )
    relay = lax.ppermute(relay, "gy", [(i, (i + 1) % count_y) for i in range(count_y)])
    norm_factor = 1.0 / math.sqrt(atoms * count_x * count_y * count_z)
    core, blocks = kernel_call(
        lambda *refs: fourth_body(*refs, norm_factor),
        (
            like((atoms, feat), full), like((count_x, tall, feat), half),
        ),
        (below_y, above_y, share, relay, core, send_y, k_kernel.T), 10**8, 8,
    )
    low, high = kernel_call(
        functools.partial(rim_body, slice(height, height + rim_y)), (like((rim_z, feat), half),) * 2,
        (below_y, above_y, table, send_z, core), 10**8, 8
    )
    below_z, above_z = swap(low, high, "gz")
    first = exchange(blocks, "gx")
    (gathered,) = kernel_call(
        functools.partial(gather_more_body, with_x, slice(height, height + rim_y)), (like((atoms, feat), full),),
        (nbr_index.T, radial, below_y, above_y, gathered), 2 * 10**9, 24,
    )
    (gathered,) = kernel_call(
        functools.partial(gather_more_body, with_y, slice(0, rim_z)), (like((atoms, feat), full),),
        (nbr_index.T, radial, below_z, above_z, gathered), 2 * 10**9, 24,
    )
    (update,) = kernel_call(
        update_body, (like((atoms, feat), half),),
        (first, core, send_x, gathered, cos_table, sin_table, w_ewald), 10**8, 16,
    )
    return update


def solution(mesh):
    in_specs = (
        P(("gx", "gy", "gz"), None),
        P(None, ("gx", "gy", "gz")),
        P(("gx", "gy", "gz"), None),
        P(("gx", "gy", "gz"), None),
        P(("gx", "gy", "gz")),
        P(None, ("gx", "gy", "gz")),
        P(None, ("gx", "gy", "gz")),
        P(None, ("gx", "gy", "gz")),
        P(),
        P(),
        P(),
        P(),
        P(),
        P(),
    )
    out_specs = P(("gx", "gy", "gz"), None)
    return jax.shard_map(
        on_device, mesh=mesh, in_specs=in_specs, out_specs=out_specs, check_vma=False
    )
```
